1024 devices in a mesh: expert: 64 (over z, core), tensor: 16 (over x, y).
Axes of the slice: x: 4, y: 4, z: 32, core: 2. Of those that a mesh axis runs over, the one named last changes fastest.
Arguments:
- cotangent: bfloat16 [4096, 4096], P('expert', 'tensor'), may hold values from -6 to 6
- activations: bfloat16 [4096, 4096], P('expert', 'tensor'), may hold values from -6 to 6
- router_logits: float32 [4096, 16], P('expert'), may hold values from -195 to 195
- saved_hidden: bfloat16 [512, 262144], P(None, ('expert', 'tensor')), may hold values from -0.046875 to 0.046875
- down_weight: bfloat16 [262144, 4096], P(('expert', 'tensor')), may hold values from -0.09375 to 0.09375
- router_weight: bfloat16 [4096, 16], P('tensor'), may hold values from -1.5 to 1.5
- choices: int32 [16, 512], replicated, may hold values from 0 to 4095, as said below
Outputs:
- hidden_grad: bfloat16 [512, 262144], P(None, ('expert', 'tensor'))
- token_grad: bfloat16 [4096, 4096], P('expert', 'tensor')
- router_grad: float32 [4096, 16], P('tensor')
The draws below stay inside these ranges and needn't reach their ends.
Inputs may be any that keep to these rules, and one draw needn't show every extreme that they name: `choices`: each row names 512 different tokens. Of the 64 tokens o * 64 to (o + 1) * 64 - 1 of one index o of expert, a row names at most 16, and every row names exactly 16 from some index.
All inputs are finite; a program needn't handle non-finite values.
Results may differ from the reference program's by a relative error of at most 0.0075.
Values may be sent and summed in bfloat16 or wider, within the bound.
A program may use at most 32 MiB of HBM per device.

```python
import jax
import jax.numpy as jnp
from jax import lax

D = 4096
FF = 16384
TOK_DEV = 64
EXPERTS = 16
TOKENS = 4096
CAP = 512
N_EXPERT = 64


def draw_router_logits(key, part):
    key = jax.random.fold_in(key, 5)
    first = jax.random.fold_in(key, 0)
    values = 3.0 * jax.random.normal(first, (TOKENS, EXPERTS), jnp.float32)
    return jnp.clip(values, -195.0, 195.0)


def draw_choices(key, part):
    key = jax.random.fold_in(key, 11)
    base_count = CAP // N_EXPERT
    spread = min(base_count, TOK_DEV - base_count)
    half_count = N_EXPERT // 2

    def one_expert(sub_key):
        key_order, key_delta, key_ranks, key_shuffle = jax.random.split(sub_key, 4)
        order = jax.random.permutation(key_order, N_EXPERT)
        delta = jax.random.randint(key_delta, (half_count,), 0, spread + 1)
        delta = delta.at[0].set(spread)
        signed = jnp.concatenate([delta, -delta])
        counts = jnp.zeros((N_EXPERT,), jnp.int32).at[order].set(base_count + signed)
        ranks = jax.vmap(lambda rank_key: jax.random.permutation(rank_key, TOK_DEV))(jax.random.split(key_ranks, N_EXPERT))
        taken = (ranks < counts[:, None]).reshape(-1)
        token_ids = jnp.arange(TOKENS, dtype=jnp.int32)
        keyed = jnp.where(taken, token_ids, TOKENS + token_ids)
        picked = jnp.sort(keyed)[:CAP]
        return jax.random.permutation(key_shuffle, picked)
    return jax.vmap(one_expert)(jax.random.split(key, EXPERTS)).astype(jnp.int32)


def steps_of(rng, shape, shards, least, largest):
    loudness = 1.0
    for axis_at, shards_of in shards:
        draws = jax.random.uniform(jax.random.fold_in(jax.random.fold_in(rng, 6), axis_at), (shards_of,), jnp.float32, least / len(shards), largest / len(shards))
        loudness = loudness * jnp.repeat(jnp.exp(draws), shape[axis_at] // shards_of).reshape((-1,) + (1,) * (len(shape) - 1 - axis_at))
    return loudness


def scatter_about(rng, shape, deviation, most, cuts=(), kind=jnp.bfloat16):
    entries = deviation * jax.random.normal(rng, shape, jnp.float32)
    if cuts:
        entries = entries * steps_of(rng, shape, cuts, -0.22, 0.18)
    return jnp.clip(entries, -most, most).astype(kind)


def setup_inputs(seed: int = 0) -> dict:
    streams_of = jax.random.split(jax.random.key(seed), 8)
    return {
        "cotangent": scatter_about(streams_of[0], (TOKENS, D), 1.0, 6.0, ((0, 64), (1, 16))),
        "activations": scatter_about(streams_of[1], (TOKENS, D), 1.0, 6.0, ((0, 64), (1, 16))),
        "router_logits": draw_router_logits(jax.random.fold_in(streams_of[7], 71), 0),
        "saved_hidden": scatter_about(streams_of[3], (CAP, EXPERTS * FF), FF ** -0.5, 0.046875, ((1, 1024),)),
        "down_weight": scatter_about(streams_of[4], (EXPERTS * FF, D), D ** -0.5, 0.09375, ((0, 1024),)),
        "router_weight": scatter_about(streams_of[5], (D, EXPERTS), EXPERTS ** -0.5, 1.5, ((0, 16),)),
        "choices": draw_choices(jax.random.fold_in(streams_of[7], 71), 0),
    }


def reference(cotangent, activations, router_logits, saved_hidden, down_weight, router_weight, choices):
    router_probs = jax.nn.softmax(router_logits, axis=1)

    def per_expert(expert):
        chosen = choices[expert]
        picked = jnp.take(cotangent, chosen, axis=0)
        weights = lax.dynamic_slice_in_dim(down_weight, expert * FF, FF, 0)
        pre_gate = lax.dot_general(picked, weights, (((1,), (1,)), ((), ())), preferred_element_type=jnp.float32)
        saved_block = lax.dynamic_slice_in_dim(saved_hidden, expert * FF, FF, 1)
        gate_grad = jnp.sum(saved_block.astype(jnp.float32) * pre_gate, axis=1)
        gate_bf = router_probs[chosen, expert].astype(jnp.bfloat16)
        scaled = (gate_bf.astype(jnp.float32)[:, None] * pre_gate).astype(jnp.bfloat16)
        return scaled, gate_grad

    scaled_all, gate_grads = lax.map(per_expert, jnp.arange(EXPERTS, dtype=jnp.int32))
    hidden_grad = jnp.transpose(scaled_all, (1, 0, 2)).reshape(CAP, EXPERTS * FF)
    expert_ids = jnp.broadcast_to(jnp.arange(EXPERTS, dtype=jnp.int32)[:, None], (EXPERTS, CAP))
    score_grad = jnp.zeros((TOKENS, EXPERTS), jnp.float32).at[choices, expert_ids].add(gate_grads)
    inner_sum = jnp.sum(router_probs * score_grad, axis=1, keepdims=True)
    logit_grad = (router_probs * (score_grad - inner_sum)).astype(jnp.bfloat16)
    token_grad = lax.dot_general(logit_grad, router_weight, (((1,), (1,)), ((), ())), preferred_element_type=jnp.float32).astype(jnp.bfloat16)
    router_grad = lax.dot_general(activations, logit_grad, (((0,), (0,)), ((), ())), preferred_element_type=jnp.float32)
    return hidden_grad, token_grad, router_grad
```

```python
import functools

import jax
import jax.numpy as jnp
from jax import lax
from jax.experimental import pallas as pl
from jax.experimental.pallas import tpu as pltpu
from jax.sharding import PartitionSpec as P

MESH = pl.DeviceIdType.MESH
F32 = jnp.float32
BF16 = jnp.bfloat16
I32 = jnp.int32
SLOTS = 16
SIDE = 4
LANES = 128
NT = (((1,), (1,)), ((), ()))
TN = (((0,), (0,)), ((), ()))
NN = (((1,), (0,)), ((), ()))


def iota(shape, axis):
    return lax.broadcasted_iota(I32, shape, axis)


def dot(a, b, dims=NN, precision=None):
    return lax.dot_general(a, b, dims, precision=precision, preferred_element_type=F32)


def exact(a, b, dims=NN):
    return dot(a, b, dims, lax.Precision.HIGHEST)


def thirds(v):
    a = v.astype(BF16).astype(F32)
    b = (v - a).astype(BF16).astype(F32)
    return a, b, v - a - b


def stack3(v, rows):
    return jnp.concatenate([t.astype(BF16) for t in thirds(v)], axis=0)


def kernel(
    cot_ref, act_ref, logit_ref, saved_ref, w_ref, rw_ref, choice_ref,
    hid_ref, tok_ref, rg_ref,
    cot_out, act_out, p_out, cot_own, cot_pair, act_own, p_own, p_pair,
    hot_own, hot_pair, xbuf, w_self, w_other, acc_self, acc_other, part_in,
    gate_xy, gate_quarter, s_out, s_in, r_out, r_in, f_out, f_in,
    w_sem, w_send, w_recv, z_send, cot_recv, act_recv, p_recv, pair_send, pair_recv,
    x_send, x_one, x_two, core_send, core_recv, g_send, g_recv, q_send, q_recv,
    s_send, s_recv, r_send, r_recv, f_send, f_recv,
):
    me, xy = lax.axis_index("expert"), lax.axis_index("tensor")
    groups = lax.axis_size("expert")
    chips = groups // 2
    experts, cap = choice_ref.shape
    z, h = me // 2, me % 2
    e = z // 2
    x, y = xy // SIDE, xy % SIDE
    own_tokens = cot_ref.shape[0]
    other_core = z * 2 + (1 - h)
    pair_z = z + 1 - 2 * (z % 2)
    quarter = (z % 2) * 2 + h
    quarters = (other_core, pair_z * 2 + h, pair_z * 2 + (1 - h))

    def remote(src, dst, send, recv, expert_at, tensor_at):
        return pltpu.make_async_remote_copy(
            src_ref=src, dst_ref=dst, send_sem=send, recv_sem=recv,
            device_id=(expert_at, tensor_at), device_id_type=MESH,
        )

    def wait_bytes(ref, sem):
        pltpu.make_async_copy(ref, ref, sem).wait()

    def at_xy(i, j):
        return ((x + i) % SIDE) * SIDE + (y + j) % SIDE

    others_xy = [(i, j) for i in range(SIDE) for j in range(SIDE) if i or j]

    blocks = w_self.shape[0]
    for b in range(blocks):
        pltpu.make_async_copy(
            w_ref.at[:, pl.ds(pl.multiple_of(b * 2 * LANES + h * LANES, LANES), LANES)],
            w_self.at[b], w_sem,
        ).start()

    barrier = pltpu.get_barrier_semaphore()

    def greet(expert_at, tensor_at):
        pl.semaphore_signal(barrier, inc=1, device_id=(expert_at, tensor_at), device_id_type=MESH)

    def greet_column(k, carry):
        to = (z + 2 * k) % chips
        greet(to * 2, xy)
        greet(to * 2 + 1, xy)
        return carry

    lax.fori_loop(1, chips // 2, greet_column, 0)
    for q in quarters:
        greet(q, xy)
    for i, j in others_xy:
        greet(me, at_xy(i, j))

    tokens_at = iota((own_tokens, cap), 0) + me * own_tokens
    lane_expert = iota((own_tokens, LANES), 1)
    chosen = jnp.zeros((own_tokens, LANES), F32)
    for n in range(experts):
        hit = (choice_ref[n : n + 1, :] == tokens_at).astype(F32)
        chosen = jnp.where(lane_expert == n, jnp.sum(hit, axis=1, keepdims=True), chosen)
    before = (iota((own_tokens, own_tokens), 1) < iota((own_tokens, own_tokens), 0)).astype(BF16)
    place = dot(before, chosen.astype(BF16))
    wide = experts * SLOTS
    spread = (iota((LANES, wide), 1) // SLOTS == iota((LANES, wide), 0)).astype(BF16)
    chosen_wide = dot(chosen.astype(BF16), spread)
    place_wide = dot(place.astype(BF16), spread)
    slot_lane = (iota((own_tokens, wide), 1) % SLOTS).astype(F32)
    pick = jnp.where((chosen_wide > 0.5) & (place_wide == slot_lane), 1.0, 0.0)
    pick_bf = pick.astype(BF16)
    logits = logit_ref[...]
    grown = jnp.exp(logits - jnp.max(logits, axis=1, keepdims=True))
    probs = grown / jnp.sum(grown, axis=1, keepdims=True)
    copies = (iota((experts, LANES), 1) % experts == iota((experts, LANES), 0)).astype(F32)
    p_terms = thirds(exact(probs, copies))
    term = iota((own_tokens, LANES), 1) // experts
    p_wide = jnp.where(
        term == 0, p_terms[0], jnp.where(term == 1, p_terms[1], jnp.where(term == 2, p_terms[2], 0.0))
    )
    cot_slots = dot(pick_bf, cot_ref[...], TN).astype(BF16)
    cot_out[0] = cot_slots[:, :LANES]
    cot_out[1] = cot_slots[:, LANES:]
    act_slots = dot(pick_bf, act_ref[...], TN).astype(BF16)
    act_out[0] = act_slots[:, :LANES]
    act_out[1] = act_slots[:, LANES:]
    p_out[...] = dot(pick_bf, p_wide.astype(BF16), TN).astype(BF16)

    pl.semaphore_wait(barrier, (chips // 2 - 1) * 2 + len(quarters) + len(others_xy))

    row = pl.multiple_of(e * 2 * SLOTS + h * SLOTS, SLOTS)

    def dispatch(out, into, recv):
        def one(k):
            to = (z + 2 * k) % chips
            rows = pl.ds(pl.multiple_of((to // 2) * SLOTS, SLOTS), SLOTS)
            for c in range(2):
                remote(
                    out(c).at[rows], into.at[pl.ds(row, SLOTS)], z_send, recv, to * 2 + c, xy
                ).start()

        far = chips // 4
        one(far)

        def near(j, carry):
            one(far - j)
            one(far + j)
            return carry

        lax.fori_loop(1, far, near, 0)
        mine = pl.ds(pl.multiple_of(e * SLOTS, SLOTS), SLOTS)
        remote(out(1 - h).at[mine], into.at[pl.ds(row, SLOTS)], z_send, recv, other_core, xy).start()
        pltpu.make_async_copy(out(h).at[mine], into.at[pl.ds(row, SLOTS)], recv).start()

    dispatch(lambda c: cot_out.at[c], cot_own, cot_recv)

    for b in range(blocks):
        remote(
            w_ref.at[:, pl.ds(pl.multiple_of(b * 2 * LANES + (1 - h) * LANES, LANES), LANES)],
            w_other.at[b], w_send, w_recv, other_core, xy,
        ).start()

    wanted = choice_ref[pl.ds(e, 1), :].astype(F32)
    wanted_row = jnp.broadcast_to(wanted, (LANES, cap))
    wanted_col = jnp.broadcast_to(jnp.transpose(wanted_row)[:, :1], (cap, cap)).astype(I32)
    wanted_row = jnp.broadcast_to(wanted, (cap, cap)).astype(I32)
    earlier = (wanted_row // own_tokens == wanted_col // own_tokens) & (wanted_row < wanted_col)
    rank = jnp.sum(earlier.astype(F32), axis=1, keepdims=True).astype(I32)
    owner = wanted_col // own_tokens
    slot = (owner // 4) * (2 * SLOTS) + (owner % 2) * SLOTS + rank
    same = slot == iota((cap, cap), 1)
    parity = (owner // 2) % 2
    hot_own[...] = (same & (parity == z % 2)).astype(BF16)
    hot_pair[...] = (same & (parity != z % 2)).astype(BF16)

    wait_bytes(cot_own, cot_recv)
    to_pair = remote(cot_own, cot_pair, pair_send.at[0], pair_recv.at[0], pair_z * 2 + h, xy)
    to_pair.start()
    picked = dot(hot_own[...], cot_own[...])
    to_pair.wait_recv()
    xbuf[xy] = (picked + dot(hot_pair[...], cot_pair[...])).astype(BF16)

    half = cap // 2
    order = (1, 3, 2)
    one_step = []

    def rows_of(first):
        return pl.ds(first * half, half)

    def along(first, i, j):
        return at_xy(i, j) if first == 0 else at_xy(j, i)

    def send_block(first, block, recv, i, j):
        ref = xbuf.at[block, rows_of(first)]
        copy = remote(ref, ref, x_send, recv, me, along(first, i, j))
        copy.start()
        return copy

    for i in order:
        for first in range(2):
            send_block(first, xy, x_one.at[first, i], i, 0)
    for j in order:
        for first in range(2):
            send_block(first, xy, x_two.at[first, 0, j], 0, j)

    dispatch(lambda c: act_out.at[c], act_own, act_recv)
    dispatch(lambda c: p_out, p_own, p_recv)

    for i in order:
        for first in range(2):
            block = along(first, -i, 0)
            wait_bytes(xbuf.at[block, rows_of(first)], x_one.at[first, i])
            for j in order:
                send_block(first, block, x_two.at[first, i, j], 0, j)

    wait_bytes(w_self, w_sem)
    wait_bytes(w_other, w_recv)

    def product(first, blocks_at, weights):
        lhs = jnp.concatenate([xbuf[b, first * half : (first + 1) * half, :] for b in blocks_at], axis=1)
        rhs = jnp.concatenate([weights[b] for b in blocks_at], axis=1)
        return dot(lhs, rhs, NT)

    def span(first):
        return slice(first * half, (first + 1) * half)

    for first in range(2):
        at = [along(first, -i, 0) for i in range(SIDE)]
        acc_other[span(first), :] = product(first, at, w_other)
        acc_self[span(first), :] = product(first, at, w_self)
    for j in order:
        last = j == order[-1]
        for first in range(2):
            at = [along(first, -i, -j) for i in range(SIDE)]
            for i in range(SIDE):
                wait_bytes(xbuf.at[at[i], rows_of(first)], x_two.at[first, i, j])
            acc_other[span(first), :] += product(first, at, w_other)
            if last:
                remote(
                    acc_other.at[rows_of(first)], part_in.at[rows_of(first)], core_send, core_recv.at[first],
                    other_core, xy,
                ).start()
            else:
                acc_self[span(first), :] += product(first, at, w_self)
    for first in range(2):
        at = [along(first, -i, -order[-1]) for i in range(SIDE)]
        acc_self[span(first), :] += product(first, at, w_self)
    for first in range(2):
        wait_bytes(part_in.at[rows_of(first)], core_recv.at[first])
    pre = acc_self[...] + part_in[...]
    acc_self[...] = pre

    gate = exact(jnp.ones((8, saved_ref.shape[1]), F32), saved_ref[...].astype(F32) * pre, NT)
    pieces = cap // LANES
    for k in range(pieces):
        gate_xy[xy, k : k + 1, :] = gate[0:1, k * LANES : (k + 1) * LANES]
    for i, j in others_xy:
        remote(gate_xy.at[xy], gate_xy.at[xy], g_send, g_recv, me, at_xy(i, j)).start()

    wait_bytes(p_own, p_recv)
    p_to_pair = remote(p_own, p_pair, pair_send.at[1], pair_recv.at[1], pair_z * 2 + h, xy)
    p_to_pair.start()
    select = (iota((experts, LANES), 1) % experts == iota((experts, LANES), 0)) & (
        iota((experts, LANES), 1) < 3 * experts
    )
    p_slot = dot(select.astype(BF16), p_own[...], NT)
    mine = iota((experts, cap), 0) == e
    p_mine = jnp.sum(jnp.where(mine, p_slot, 0.0), axis=0, keepdims=True)
    slope = p_mine * (jnp.where(mine, 1.0, 0.0) - p_slot)
    wait_bytes(act_own, act_recv)

    wait_bytes(gate_xy.at[pl.ds(0, len(others_xy))], g_recv)
    gate_quarter[quarter] = jnp.sum(gate_xy[...], axis=0)
    for q in quarters:
        remote(gate_quarter.at[quarter], gate_quarter.at[quarter], q_send, q_recv, q, xy).start()
    wait_bytes(gate_quarter.at[pl.ds(0, len(quarters))], q_recv)
    total = jnp.sum(gate_quarter[...], axis=0)
    total_row = jnp.concatenate([total[k : k + 1, :] for k in range(pieces)], axis=1)
    rows3 = jnp.concatenate([total_row, jnp.zeros((7, cap), F32)], axis=0)
    s_three = dot(jnp.concatenate(thirds(rows3), axis=0).astype(BF16), hot_own[...])
    s_slot = s_three[0:1] + s_three[8:9] + s_three[16:17]

    slot_at = iota((experts, cap), 1)
    of_owner = (slot_at // (2 * SLOTS) == iota((experts, cap), 0)) & ((slot_at // SLOTS) % 2 == h)
    fold = (iota((cap, LANES), 0) % SLOTS == iota((cap, LANES), 1)).astype(F32)
    s_rows = exact(jnp.where(of_owner, s_slot, 0.0), fold)
    for k in range(experts):
        s_out[k] = s_rows[k : k + 1, :]
    w_slot = s_slot * slope
    r_three = dot(jnp.concatenate(thirds(w_slot), axis=0).astype(BF16), act_own[...])
    r_part = r_three[:experts] + r_three[experts : 2 * experts] + r_three[2 * experts :]
    r_out[...] = r_part.astype(BF16)

    def back(out, into, send, recv):
        def one(k):
            to = (z + 2 * k) % chips
            remote(out(to // 2), into.at[e], send, recv, to * 2 + h, xy).start()

        far = chips // 4
        one(far)

        def near(j, carry):
            one(far - j)
            one(far + j)
            return carry

        lax.fori_loop(1, far, near, 0)

    back(lambda k: s_out.at[k], s_in, s_send, s_recv)
    back(lambda k: r_out, r_in, r_send, r_recv)
    s_in[e] = s_out[e]
    r_in[e] = r_out[...]

    p_to_pair.wait_recv()
    gates = dot(hot_own[...], p_own[...]) + dot(hot_pair[...], p_pair[...])
    gate_col = jnp.sum(jnp.where(iota((cap, LANES), 1) == e, gates, 0.0), axis=1, keepdims=True)
    hid_ref[...] = (gate_col * acc_self[...]).astype(BF16)

    wait_bytes(s_in.at[pl.ds(0, experts - 1)], s_recv)
    s_all = jnp.concatenate([s_in[k] for k in range(experts)], axis=0)
    unfold = (iota((LANES, wide), 1) % SLOTS == iota((LANES, wide), 0)).astype(F32)
    own_lane = iota((experts, wide), 1) // SLOTS == iota((experts, wide), 0)
    s_wide = jnp.where(own_lane, exact(s_all, unfold), 0.0)
    score = exact(pick, s_wide, NT)
    inner = jnp.sum(probs * score, axis=1, keepdims=True)
    logit_grad = (probs * (score - inner)).astype(BF16)
    tok_ref[...] = dot(logit_grad, rw_ref[...], NT).astype(BF16)

    wait_bytes(r_in.at[pl.ds(0, experts - 1)], r_recv)
    f_out[...] = jnp.sum(r_in[...].astype(F32), axis=0)
    f_in[quarter] = f_out[...]
    for q in quarters:
        remote(f_out, f_in.at[quarter], f_send, f_recv, q, xy).start()
    wait_bytes(f_in.at[pl.ds(0, len(quarters))], f_recv)
    left = f_in[0] + f_in[2]
    right = f_in[1] + f_in[3]
    both = jnp.concatenate([left, right], axis=1)
    both = jnp.concatenate([both, jnp.zeros((LANES - experts, both.shape[1]), F32)], axis=0)
    rg_ref[...] = jnp.transpose(both)[:, :experts]

    for ref in (w_other, part_in):
        pass
    wait_bytes(w_other, w_send)
    def sent(ref):
        pltpu.make_async_copy(ref, ref, z_send).wait()

    for ref in (cot_own, act_own, p_own):
        sent(ref.at[pl.ds(0, cap - SLOTS)])
    to_pair.wait_send()
    p_to_pair.wait_send()
    for _ in range(15):
        wait_bytes(xbuf.at[0], x_send)
    wait_bytes(acc_other, core_send)
    wait_bytes(gate_xy.at[pl.ds(0, len(others_xy))], g_send)
    wait_bytes(gate_quarter.at[pl.ds(0, len(quarters))], q_send)
    wait_bytes(s_in.at[pl.ds(0, experts - 1)], s_send)
    wait_bytes(r_in.at[pl.ds(0, experts - 1)], r_send)
    wait_bytes(f_in.at[pl.ds(0, len(quarters))], f_send)


def on_device(
    cotangent, activations, router_logits, saved_hidden, down_weight, router_weight, choices
):
    experts, cap = choices.shape
    own_tokens, feats = cotangent.shape
    hidden = down_weight.shape[0]
    wide = experts * SLOTS
    blocks = SIDE * SIDE
    vmem = pl.BlockSpec(memory_space=pltpu.VMEM)
    dma = pltpu.SemaphoreType.DMA
    return pl.pallas_call(
        kernel,
        out_shape=(
            jax.ShapeDtypeStruct((cap, hidden), BF16),
            jax.ShapeDtypeStruct((own_tokens, feats), BF16),
            jax.ShapeDtypeStruct((feats, experts), F32),
        ),
        in_specs=[vmem, vmem, vmem, vmem, pl.BlockSpec(memory_space=pl.ANY), vmem, vmem],
        out_specs=(vmem, vmem, vmem),
        scratch_shapes=[
            pltpu.VMEM((2, wide, LANES), BF16),
            pltpu.VMEM((2, wide, LANES), BF16),
            pltpu.VMEM((wide, LANES), BF16),
            pltpu.VMEM((cap, LANES), BF16),
            pltpu.VMEM((cap, LANES), BF16),
            pltpu.VMEM((cap, LANES), BF16),
            pltpu.VMEM((cap, LANES), BF16),
            pltpu.VMEM((cap, LANES), BF16),
            pltpu.VMEM((cap, cap), BF16),
            pltpu.VMEM((cap, cap), BF16),
            pltpu.VMEM((blocks, cap, LANES), BF16),
            pltpu.VMEM((blocks, hidden, LANES), BF16),
            pltpu.VMEM((blocks, hidden, LANES), BF16),
            pltpu.VMEM((cap, hidden), F32),
            pltpu.VMEM((cap, hidden), F32),
            pltpu.VMEM((cap, hidden), F32),
            pltpu.VMEM((blocks, cap // LANES, LANES), F32),
            pltpu.VMEM((4, cap // LANES, LANES), F32),
            pltpu.VMEM((experts, 1, LANES), F32),
            pltpu.VMEM((experts, 1, LANES), F32),
            pltpu.VMEM((experts, LANES), BF16),
            pltpu.VMEM((experts, experts, LANES), BF16),
            pltpu.VMEM((experts, LANES), F32),
            pltpu.VMEM((4, experts, LANES), F32),
            dma(()), dma(()), dma(()),
            dma(()), dma(()), dma(()), dma(()),
            dma((2,)), dma((2,)),
            dma(()), dma((2, SIDE)), dma((2, SIDE, SIDE)),
            dma(()), dma((2,)),
            dma(()), dma(()), dma(()), dma(()),
            dma(()), dma(()), dma(()), dma(()), dma(()), dma(()),
        ],
        compiler_params=pltpu.CompilerParams(
            collective_id=0, has_side_effects=True, vmem_limit_bytes=48 * 2**20
        ),
        cost_estimate=pl.CostEstimate(
            flops=2 * cap * hidden * feats * blocks, bytes_accessed=4 * 2**20, transcendentals=0
        ),
        name="gated_moe_backward",
    )(cotangent, activations, router_logits, saved_hidden, down_weight, router_weight, choices)


def solution(mesh):
    placed = (
        P("expert", "tensor"),
        P("expert", "tensor"),
        P("expert", None),
        P(None, ("expert", "tensor")),
        P(("expert", "tensor"), None),
        P("tensor", None),
        P(),
    )
    return jax.shard_map(
        on_device,
        mesh=mesh,
        in_specs=placed,
        out_specs=(P(None, ("expert", "tensor")), P("expert", "tensor"), P("tensor", None)),
        check_vma=False,
    )
```

```python
import functools

import jax
import jax.numpy as jnp
from jax import lax
from jax.experimental import pallas as pl
from jax.experimental.pallas import tpu as pltpu
from jax.sharding import PartitionSpec as P

MESH = pl.DeviceIdType.MESH
F32 = jnp.float32
BF16 = jnp.bfloat16
I32 = jnp.int32
SLOTS = 16
SIDE = 4
LANES = 128
NT = (((1,), (1,)), ((), ()))
TN = (((0,), (0,)), ((), ()))
NN = (((1,), (0,)), ((), ()))


def iota(shape, axis):
    return lax.broadcasted_iota(I32, shape, axis)


def dot(a, b, dims=NN, precision=None):
    return lax.dot_general(a, b, dims, precision=precision, preferred_element_type=F32)


def exact(a, b, dims=NN):
    return dot(a, b, dims, lax.Precision.HIGHEST)


def thirds(v):
    a = v.astype(BF16).astype(F32)
    b = (v - a).astype(BF16).astype(F32)
    return a, b, v - a - b


def shift_of(n):
    return n.bit_length() - 1


def kernel(
    cot_hbm, act_hbm, logit_hbm, saved_hbm, w_hbm, rw_hbm, choice_hbm,
    hid_ref, tok_ref, rg_ref,
    cot_ref, act_ref, logit_ref, saved_ref, saved_other, rw_ref, choice_ref,
    cot_out, act_out, p_out, up, down, cot_own, cot_pair, act_own, p_own, p_pair,
    hot_own, hot_pair, xbuf, w_self, w_other, acc_self, acc_other, part_in,
    gate_one, gate_two, s_out, s_in, r_out, r_in, f_out, f_in,
    in_sem, w_sem, w_send, w_recv, saved_send, saved_recv,
    up_send, up_recv, near_send, hop_send, cot_recv, pair_send, pair_recv,
    act_send, act_recv, p_send, p_recv, p_two_send, p_two_recv, p_pair_send, p_pair_recv,
    x_send, x_one, x_two, core_send, core_recv, one_send, one_recv, two_send, two_recv,
    s_send, s_recv, r_send, r_recv, f_send, f_recv,
):
    me, xy = lax.axis_index("expert"), lax.axis_index("tensor")
    groups = lax.axis_size("expert")
    chips = groups // 2
    experts, cap = choice_ref.shape
    own_tokens, feats = cot_ref.shape
    z, h = me // 2, me % 2
    e = z // 2
    x, y = xy // SIDE, xy % SIDE
    other_core = z * 2 + (1 - h)
    pair_z = z + 1 - 2 * (z % 2)
    pair = pair_z * 2 + h
    quarter = (z % 2) * 2 + h
    quarters = (other_core, pair, pair_z * 2 + (1 - h))
    far = 4
    token_shift, slot_shift = shift_of(own_tokens), shift_of(SLOTS)

    def remote(src, dst, send, recv, expert_at, tensor_at=xy):
        return pltpu.make_async_remote_copy(
            src_ref=src, dst_ref=dst, send_sem=send, recv_sem=recv,
            device_id=(expert_at, tensor_at), device_id_type=MESH,
        )

    def wait_bytes(ref, sem):
        pltpu.make_async_copy(ref, ref, sem).wait()

    waits = {}

    def later(name, ref, sem):
        waits[name] = lambda: wait_bytes(ref, sem)

    def finish(name):
        waits.pop(name)()

    def at_xy(i, j):
        return ((x + i) % SIDE) * SIDE + (y + j) % SIDE

    def at_z(k):
        return (z + 2 * k + 2 * chips) % chips

    arrays = {
        "choice": (choice_hbm, choice_ref), "cot": (cot_hbm, cot_ref), "act": (act_hbm, act_ref),
        "logit": (logit_hbm, logit_ref), "saved": (saved_hbm, saved_ref), "rw": (rw_hbm, rw_ref),
    }

    def load(*names):
        for name in names:
            src, dst = arrays[name]
            sem = in_sem.at[list(arrays).index(name)]
            pltpu.make_async_copy(src, dst, sem).start()
            later(name, dst, sem)

    load("choice", "cot")

    barrier = pltpu.get_barrier_semaphore()

    def greet(expert_at, tensor_at):
        pl.semaphore_signal(barrier, inc=1, device_id=(expert_at, tensor_at), device_id_type=MESH)

    near_steps = [k * sign for k in range(far, 0, -1) for sign in (1, -1)]
    for k in near_steps:
        for c in range(2):
            greet(at_z(k) * 2 + c, xy)
    for i in range(1, SIDE):
        greet(me, at_xy(0, i))
        greet(me, at_xy(i, 0))
        for q in quarters:
            greet(q, at_xy(i, 0))
    for q in quarters:
        greet(q, xy)
    greeted = 2 * len(near_steps) + 5 * (SIDE - 1) + len(quarters)

    finish("choice")
    tokens_at = iota((own_tokens, cap), 0) + me * own_tokens
    lane_expert = iota((own_tokens, LANES), 1)
    chosen = jnp.zeros((own_tokens, LANES), F32)
    for n in range(experts):
        hit = jnp.where(choice_ref[n : n + 1, :] == tokens_at, 1.0, 0.0)
        chosen = jnp.where(lane_expert == n, jnp.sum(hit, axis=1, keepdims=True), chosen)
    before = (iota((own_tokens, own_tokens), 1) < iota((own_tokens, own_tokens), 0)).astype(F32).astype(BF16)
    place = dot(before, chosen.astype(BF16))
    wide = experts * SLOTS
    group_of = (jnp.right_shift(iota((LANES, wide), 1), slot_shift) + e) & (experts - 1)
    spread = (group_of == iota((LANES, wide), 0)).astype(F32).astype(BF16)
    chosen_wide = dot(chosen.astype(BF16), spread)
    place_wide = dot(place.astype(BF16), spread)
    slot_lane = (iota((own_tokens, wide), 1) & (SLOTS - 1)).astype(F32)
    pick = jnp.where((chosen_wide > 0.5) & (place_wide == slot_lane), 1.0, 0.0)
    pick_bf = pick.astype(BF16)
    finish("cot")
    cot_slots = dot(pick_bf, cot_ref[...], TN).astype(BF16)
    cot_out[0] = cot_slots[:, :LANES].reshape(experts, SLOTS, LANES)
    cot_out[1] = cot_slots[:, LANES:].reshape(experts, SLOTS, LANES)

    pl.semaphore_wait(barrier, greeted)

    slots_of_core = pl.ds(pl.multiple_of(h * SLOTS, SLOTS), SLOTS)
    for c in range(2):
        remote(
            cot_out.at[c, pl.ds(far + 1, far - c)], up.at[pl.ds(0, far - c), slots_of_core], up_send.at[0],
            up_recv.at[0], at_z(far) * 2 + c,
        ).start()
        remote(
            cot_out.at[c, pl.ds(2 * far + 1 - c, far - 1 + c)], down.at[pl.ds(1 - c, far - 1 + c), slots_of_core],
            up_send.at[1], up_recv.at[1], at_z(-far) * 2 + c,
        ).start()
    pair_rows = 2 * SLOTS

    def rows_from(k):
        return pl.ds(pl.multiple_of(((e - k + experts) % experts) * pair_rows, pair_rows), pair_rows)

    mine = pl.ds(pl.multiple_of(e * pair_rows + h * SLOTS, SLOTS), SLOTS)
    for k in near_steps:
        for c in range(2):
            remote(
                cot_out.at[c, k % experts], cot_own.at[mine], near_send, cot_recv.at[k % experts], at_z(k) * 2 + c
            ).start()
    remote(cot_out.at[1 - h, 0], cot_own.at[mine], near_send, cot_recv.at[0], other_core).start()
    pltpu.make_async_copy(cot_out.at[h, 0], cot_own.at[mine], cot_recv.at[0]).start()
    load("act", "logit")
    later("near", cot_own.at[pl.ds(0, (2 * len(near_steps) + 1) * SLOTS)], near_send)

    blocks = w_self.shape[0]
    for b in range(blocks):
        pltpu.make_async_copy(
            w_hbm.at[:, pl.ds(pl.multiple_of(b * 2 * LANES + h * LANES, LANES), LANES)],
            w_self.at[b], w_sem,
        ).start()
    later("w", w_self, w_sem)

    load("saved", "rw")

    finish("act")
    act_slots = dot(pick_bf, act_ref[...], TN).astype(BF16)
    act_out[0] = act_slots[:, :LANES].reshape(experts, SLOTS, LANES)
    act_out[1] = act_slots[:, LANES:].reshape(experts, SLOTS, LANES)
    finish("logit")
    logits = logit_ref[...]
    grown = jnp.exp(logits - jnp.max(logits, axis=0, keepdims=True))
    probs = grown / jnp.sum(grown, axis=0, keepdims=True)
    lane = iota((experts, LANES), 1)
    copies = jnp.where((lane & (experts - 1)) == iota((experts, LANES), 0), 1.0, 0.0)
    p_terms = thirds(exact(probs, copies, TN))
    term = jnp.right_shift(iota((own_tokens, LANES), 1), shift_of(experts))
    p_wide = jnp.where(
        term == 0, p_terms[0], jnp.where(term == 1, p_terms[1], jnp.where(term == 2, p_terms[2], 0.0))
    )
    p_out[...] = dot(pick_bf, p_wide.astype(BF16), TN).astype(BF16).reshape(experts, SLOTS, LANES)

    middle = experts // 2

    def act_to(k):
        for c in range(2):
            remote(act_out.at[c, k], act_own.at[mine], act_send, act_recv, at_z(k) * 2 + c).start()

    def act_each(j, carry):
        act_to(middle - j)
        act_to(middle + j)
        return carry

    def p_to(k):
        for c in range(2):
            remote(p_out.at[k], p_own.at[mine], p_send, p_recv, at_z(k) * 2 + c).start()

    def send_rest():
        for m in range(SIDE - 1, 0, -1):
            p_to(m * SIDE + y)

        @pl.when(y != 0)
        def _():
            p_to(y)

        @pl.when(y == 0)
        def _():
            remote(p_out.at[0], p_own.at[mine], p_send, p_recv, other_core).start()
            pltpu.make_async_copy(p_out.at[0], p_own.at[mine], p_recv).start()

        act_to(middle)
        lax.fori_loop(1, middle, act_each, 0)
        remote(act_out.at[1 - h, 0], act_own.at[mine], act_send, act_recv, other_core).start()
        pltpu.make_async_copy(act_out.at[h, 0], act_own.at[mine], act_recv).start()
        later("act_send", act_own.at[pl.ds(0, cap - SLOTS)], act_send)
        later("act_slots", act_own, act_recv)
        waits["p_send"] = p_sent

    def p_sent():
        sends = 2 * experts // SIDE

        @pl.when(y == 0)
        def _():
            wait_bytes(p_own.at[pl.ds(0, (sends - 1) * SLOTS)], p_send)

        @pl.when(y != 0)
        def _():
            wait_bytes(p_own.at[pl.ds(0, sends * SLOTS)], p_send)

    def share_p():
        wait_bytes(p_own.at[pl.ds(0, cap // SIDE)], p_recv)
        for m in range(SIDE):
            rows = rows_from(m * SIDE + y)
            for j in (2, 1, 3):
                remote(p_own.at[rows], p_own.at[rows], p_two_send, p_two_recv, me, at_xy(0, j)).start()
        rest = p_own.at[pl.ds(0, cap - cap // SIDE)]
        later("p_two_send", rest, p_two_send)
        later("p_slots", rest, p_two_recv)

    def share(k):
        rows = rows_from(k)
        wait_bytes(cot_own.at[rows], cot_recv.at[k % experts])
        remote(cot_own.at[rows], cot_pair.at[rows], pair_send, pair_recv, pair).start()

    later("pair_send", cot_pair, pair_send)
    later("pair", cot_pair, pair_recv)

    def hop_up(j):
        remote(
            up.at[j], cot_own.at[rows_from(far)], hop_send.at[0], cot_recv.at[far + 1 + j], at_z(1 + j) * 2 + h
        ).start()

    def hop_down(j):
        remote(
            down.at[j], cot_own.at[rows_from(-far)], hop_send.at[1], cot_recv.at[2 * far + j], at_z(j - far) * 2 + h
        ).start()

    for k in (0, 1, -1, 2, -2):
        share(k)
    most, fewer = pl.ds(0, far), pl.ds(0, far - 1)

    @pl.when(h == 0)
    def _():
        wait_bytes(up.at[most], up_recv.at[0])
        hop_up(far - 1)

    @pl.when(h == 1)
    def _():
        wait_bytes(up.at[fewer], up_recv.at[0])

    for j in range(far - 2, -1, -1):
        hop_up(j)

    @pl.when(h == 1)
    def _():
        wait_bytes(down.at[most], up_recv.at[1])
        hop_down(0)

    @pl.when(h == 0)
    def _():
        wait_bytes(down.at[fewer], up_recv.at[1])

    for j in range(1, far):
        hop_down(j)

    def hopped():
        @pl.when(h == 0)
        def _():
            wait_bytes(up.at[most], hop_send.at[0])
            wait_bytes(down.at[fewer], hop_send.at[1])

        @pl.when(h == 1)
        def _():
            wait_bytes(up.at[fewer], hop_send.at[0])
            wait_bytes(down.at[most], hop_send.at[1])

    waits["hop"] = hopped
    relayed = cot_own.at[pl.ds(0, (2 * far - 1) * SLOTS)]
    later("up_send", relayed, up_send.at[0])
    later("down_send", relayed, up_send.at[1])

    wanted = choice_ref[pl.ds(e, 1), :].astype(F32)
    wanted_col = jnp.transpose(jnp.broadcast_to(wanted, (LANES, cap)))[:, :1].astype(I32)
    wanted_row = wanted.astype(I32)
    owner_col = jnp.right_shift(wanted_col, token_shift)
    owner_row = jnp.right_shift(wanted_row, token_shift)
    earlier = (owner_row == owner_col) & (wanted_row < wanted_col)
    rank = jnp.sum(jnp.where(earlier, 1.0, 0.0), axis=1, keepdims=True).astype(I32)
    slot = jnp.right_shift(owner_col, 2) * pair_rows + (owner_col & 1) * SLOTS + rank
    ours = (jnp.right_shift(owner_col, 1) & 1) == z % 2
    slot_lanes = iota((cap, cap), 1)
    hot_own[...] = jnp.where(jnp.where(ours, slot, -1) == slot_lanes, 1.0, 0.0).astype(BF16)
    hot_pair[...] = jnp.where(jnp.where(ours, -1, slot) == slot_lanes, 1.0, 0.0).astype(BF16)

    for k in (3, -3, 4, -4, 5, -5, 6, -6, 7, -7, 8):
        share(k)
    picked = dot(hot_own[...], cot_own[...])
    finish("pair")
    xbuf[xy] = (picked + dot(hot_pair[...], cot_pair[...])).astype(BF16)

    half = cap // 2
    order = (1, 3, 2)

    def rows_of(first):
        return pl.ds(first * half, half)

    def along(first, i, j):
        return at_xy(i, j) if first == 0 else at_xy(j, i)

    def send_block(first, block, recv, i, j):
        ref = xbuf.at[block, rows_of(first)]
        remote(ref, ref, x_send, recv, me, along(first, i, j)).start()

    for i in order:
        for first in range(2):
            send_block(first, xy, x_one.at[first, i], i, 0)
    for j in order:
        for first in range(2):
            send_block(first, xy, x_two.at[first, 0, j], 0, j)
    for b in range(blocks):
        remote(
            w_hbm.at[:, pl.ds(pl.multiple_of(b * 2 * LANES + (1 - h) * LANES, LANES), LANES)],
            w_other.at[b], w_send, w_recv, other_core,
        ).start()
    later("w_send", w_other, w_send)
    later("w_other", w_other, w_recv)
    remote(saved_hbm, saved_other, saved_send, saved_recv, other_core).start()
    later("saved_send", saved_other, saved_send)
    later("saved_other", saved_other, saved_recv)

    later("x_send", xbuf.at[pl.ds(0, SIDE * SIDE - 1)], x_send)

    def relay(i):
        for first in range(2):
            block = along(first, -i, 0)
            wait_bytes(xbuf.at[block, rows_of(first)], x_one.at[first, i])
            for j in order:
                send_block(first, block, x_two.at[first, i, j], 0, j)

    send_rest()
    relay(1)
    relay(3)
    relay(2)
    share_p()

    finish("w")
    finish("w_other")

    def product(first, blocks_at, weights):
        lhs = jnp.concatenate([xbuf[b, first * half : (first + 1) * half, :] for b in blocks_at], axis=1)
        rhs = jnp.concatenate([weights[b] for b in blocks_at], axis=1)
        return dot(lhs, rhs, NT)

    def span(first):
        return slice(first * half, (first + 1) * half)

    for first in range(2):
        at = [along(first, -i, 0) for i in range(SIDE)]
        acc_other[span(first), :] = product(first, at, w_other)
        acc_self[span(first), :] = product(first, at, w_self)
    for j in order:
        for first in range(2):
            at = [along(first, -i, -j) for i in range(SIDE)]
            for i in range(SIDE):
                wait_bytes(xbuf.at[at[i], rows_of(first)], x_two.at[first, i, j])
            acc_other[span(first), :] += product(first, at, w_other)
            acc_self[span(first), :] += product(first, at, w_self)

    finish("saved")
    finish("saved_other")
    prod = saved_ref[...].astype(F32) * acc_self[...] + saved_other[...].astype(F32) * acc_other[...]
    gate = jnp.sum(jnp.transpose(prod[:, :LANES] + prod[:, LANES:]), axis=0, keepdims=True)
    pieces = cap // LANES
    slot_one = x * 4 + quarter
    for k in range(pieces):
        gate_one[slot_one, k : k + 1, :] = gate[0:1, k * LANES : (k + 1) * LANES]
    for i in (2, 1, 3, 0):
        for q in quarters + (() if i == 0 else (me,)):
            remote(gate_one.at[slot_one], gate_one.at[slot_one], one_send, one_recv, q, at_xy(i, 0)).start()
    later("one_send", gate_one.at[pl.ds(0, 4 * SIDE - 1)], one_send)
    wait_bytes(gate_one.at[pl.ds(0, 4 * SIDE - 1)], one_recv)
    gate_two[y] = jnp.sum(gate_one[...], axis=0)
    for j in (2, 1, 3):
        remote(gate_two.at[y], gate_two.at[y], two_send, two_recv, me, at_xy(0, j)).start()
    later("two_send", gate_two.at[pl.ds(0, SIDE - 1)], two_send)

    for first in range(2):
        remote(
            acc_other.at[rows_of(first)], part_in.at[rows_of(first)], core_send, core_recv, other_core
        ).start()
    later("core_send", acc_other, core_send)
    later("part", part_in, core_recv)

    finish("p_slots")
    p_to_pair = remote(p_own, p_pair, p_pair_send, p_pair_recv, pair)
    p_to_pair.start()
    later("p_pair_send", p_pair, p_pair_send)
    later("p_pair", p_pair, p_pair_recv)
    select = jnp.where(lane < 3 * experts, copies, 0.0)
    p_slot = dot(select.astype(BF16), p_own[...], NT)
    mine_row = iota((experts, cap), 0) == e
    p_mine = jnp.sum(jnp.where(mine_row, p_slot, 0.0), axis=0, keepdims=True)
    slope = p_mine * (jnp.where(mine_row, 1.0, 0.0) - p_slot)
    finish("act_slots")

    wait_bytes(gate_two.at[pl.ds(0, SIDE - 1)], two_recv)
    total = jnp.sum(gate_two[...], axis=0)
    total_row = jnp.concatenate([total[k : k + 1, :] for k in range(pieces)], axis=1)
    rows3 = jnp.concatenate([total_row, jnp.zeros((7, cap), F32)], axis=0)
    s_three = dot(jnp.concatenate(thirds(rows3), axis=0).astype(BF16), hot_own[...])
    s_slot = s_three[0:1] + s_three[8:9] + s_three[16:17]

    def back(name, out, into, send, recv):
        def one(k):
            to = (z + 2 * k) % chips
            remote(out(to // 2), into.at[e], send, recv, to * 2 + h).start()

        middle = experts // 2
        one(middle)

        def each(j, carry):
            one(middle - j)
            one(middle + j)
            return carry

        lax.fori_loop(1, middle, each, 0)
        later(name + "_send", into.at[pl.ds(0, experts - 1)], send)
        later(name, into.at[pl.ds(0, experts - 1)], recv)

    w_slot = s_slot * slope
    r_three = dot(jnp.concatenate(thirds(w_slot), axis=0).astype(BF16), act_own[...])
    r_part = r_three[:experts] + r_three[experts : 2 * experts] + r_three[2 * experts :]
    r_out[...] = r_part.astype(BF16)
    back("r", lambda k: r_out, r_in, r_send, r_recv)
    slot_at = iota((experts, cap), 1)
    of_owner = (jnp.right_shift(slot_at, slot_shift + 1) == iota((experts, cap), 0)) & (
        (jnp.right_shift(slot_at, slot_shift) & 1) == h
    )
    fold = jnp.where((iota((cap, LANES), 0) & (SLOTS - 1)) == iota((cap, LANES), 1), 1.0, 0.0)
    s_spread = jnp.concatenate(thirds(jnp.where(of_owner, s_slot, 0.0)), axis=0).astype(BF16)
    s_three = dot(s_spread, fold.astype(BF16))
    s_rows = s_three[:experts] + s_three[experts : 2 * experts] + s_three[2 * experts :]
    for k in range(experts):
        s_out[k] = s_rows[k : k + 1, :]

    back("s", lambda k: s_out.at[k], s_in, s_send, s_recv)
    r_in[e] = r_out[...]
    s_in[e] = s_out[e]

    finish("p_pair")
    gates = dot(hot_own[...], p_own[...]) + dot(hot_pair[...], p_pair[...])
    gate_col = jnp.sum(jnp.where(iota((cap, LANES), 1) == e, gates, 0.0), axis=1, keepdims=True)
    finish("part")
    hid_ref[...] = (gate_col * (acc_self[...] + part_in[...])).astype(BF16)

    finish("rw")
    finish("s")
    s_all = jnp.concatenate([s_in[k] for k in range(experts)], axis=0)
    unfold = jnp.where((iota((LANES, wide), 1) & (SLOTS - 1)) == iota((LANES, wide), 0), 1.0, 0.0)
    s_three = dot(jnp.concatenate(thirds(s_all), axis=0).astype(BF16), unfold.astype(BF16))
    s_sum = s_three[:experts] + s_three[experts : 2 * experts] + s_three[2 * experts :]
    own_lane = ((jnp.right_shift(iota((experts, wide), 1), slot_shift) + e) & (experts - 1)) == iota((experts, wide), 0)
    score3 = dot(jnp.concatenate(thirds(jnp.where(own_lane, s_sum, 0.0)), axis=0).astype(BF16), pick_bf, NT)
    score = score3[:experts] + score3[experts : 2 * experts] + score3[2 * experts :]
    inner = jnp.sum(probs * score, axis=0, keepdims=True)
    logit_grad = (probs * (score - inner)).astype(BF16)
    tok_ref[...] = dot(logit_grad, rw_ref[...], TN).astype(BF16)

    finish("r")
    f_out[...] = jnp.sum(r_in[...].astype(F32), axis=0)
    f_in[quarter] = f_out[...]
    for q in quarters:
        remote(f_out, f_in.at[quarter], f_send, f_recv, q).start()
    later("f_send", f_in.at[pl.ds(0, len(quarters))], f_send)
    wait_bytes(f_in.at[pl.ds(0, len(quarters))], f_recv)
    rg_ref[:, :LANES] = f_in[0] + f_in[2]
    rg_ref[:, LANES:] = f_in[1] + f_in[3]

    for name in list(waits):
        finish(name)


def on_device(
    cotangent, activations, router_logits, saved_hidden, down_weight, router_weight, choices
):
    experts, cap = choices.shape
    own_tokens, feats = cotangent.shape
    hidden = down_weight.shape[0]
    wide = experts * SLOTS
    blocks = SIDE * SIDE
    vmem = pl.BlockSpec(memory_space=pltpu.VMEM)
    hbm = pl.BlockSpec(memory_space=pltpu.HBM)
    dma = pltpu.SemaphoreType.DMA
    hidden_grad, token_grad, router_grad = pl.pallas_call(
        kernel,
        out_shape=(
            jax.ShapeDtypeStruct((cap, hidden), BF16),
            jax.ShapeDtypeStruct((own_tokens, feats), BF16),
            jax.ShapeDtypeStruct((experts, feats), F32),
        ),
        in_specs=[hbm] * 7,
        out_specs=(vmem, vmem, vmem),
        scratch_shapes=[
            pltpu.VMEM((own_tokens, feats), BF16),
            pltpu.VMEM((own_tokens, feats), BF16),
            pltpu.VMEM((experts, own_tokens), F32),
            pltpu.VMEM((cap, hidden), BF16),
            pltpu.VMEM((cap, hidden), BF16),
            pltpu.VMEM((experts, feats), BF16),
            pltpu.VMEM((experts, cap), I32),
            pltpu.VMEM((2, experts, SLOTS, LANES), BF16),
            pltpu.VMEM((2, experts, SLOTS, LANES), BF16),
            pltpu.VMEM((experts, SLOTS, LANES), BF16),
            pltpu.VMEM((4, 2 * SLOTS, LANES), BF16),
            pltpu.VMEM((4, 2 * SLOTS, LANES), BF16),
            pltpu.VMEM((cap, LANES), BF16),
            pltpu.VMEM((cap, LANES), BF16),
            pltpu.VMEM((cap, LANES), BF16),
            pltpu.VMEM((cap, LANES), BF16),
            pltpu.VMEM((cap, LANES), BF16),
            pltpu.VMEM((cap, cap), BF16),
            pltpu.VMEM((cap, cap), BF16),
            pltpu.VMEM((blocks, cap, LANES), BF16),
            pltpu.VMEM((blocks, hidden, LANES), BF16),
            pltpu.VMEM((blocks, hidden, LANES), BF16),
            pltpu.VMEM((cap, hidden), F32),
            pltpu.VMEM((cap, hidden), F32),
            pltpu.VMEM((cap, hidden), F32),
            pltpu.VMEM((4 * SIDE, cap // LANES, LANES), F32),
            pltpu.VMEM((SIDE, cap // LANES, LANES), F32),
            pltpu.VMEM((experts, 1, LANES), F32),
            pltpu.VMEM((experts, 1, LANES), F32),
            pltpu.VMEM((experts, LANES), BF16),
            pltpu.VMEM((experts, experts, LANES), BF16),
            pltpu.VMEM((experts, LANES), F32),
            pltpu.VMEM((4, experts, LANES), F32),
            dma((6,)), dma(()), dma(()), dma(()), dma(()), dma(()),
            dma((2,)), dma((2,)), dma(()), dma((2,)), dma((experts,)), dma(()), dma(()),
            dma(()), dma(()), dma(()), dma(()), dma(()), dma(()), dma(()), dma(()),
            dma(()), dma((2, SIDE)), dma((2, SIDE, SIDE)), dma(()), dma(()),
            dma(()), dma(()), dma(()), dma(()),
            dma(()), dma(()), dma(()), dma(()), dma(()), dma(()),
        ],
        compiler_params=pltpu.CompilerParams(
            collective_id=0, has_side_effects=True, vmem_limit_bytes=48 * 2**20
        ),
        cost_estimate=pl.CostEstimate(
            flops=2 * cap * hidden * feats * blocks, bytes_accessed=4 * 2**20, transcendentals=0
        ),
        name="gated_moe_backward",
    )(
        *(
            pltpu.with_memory_space_constraint(v, pltpu.HBM)
            for v in (
                cotangent, activations, router_logits.T, saved_hidden, down_weight, router_weight.T, choices
            )
        )
    )
    return hidden_grad, token_grad, router_grad.T


def solution(mesh):
    placed = (
        P("expert", "tensor"),
        P("expert", "tensor"),
        P("expert", None),
        P(None, ("expert", "tensor")),
        P(("expert", "tensor"), None),
        P("tensor", None),
        P(),
    )
    return jax.shard_map(
        on_device,
        mesh=mesh,
        in_specs=placed,
        out_specs=(P(None, ("expert", "tensor")), P("expert", "tensor"), P("tensor", None)),
        check_vma=False,
    )
```

```python
import functools

import jax
import jax.numpy as jnp
from jax import lax
from jax.experimental import pallas as pl
from jax.experimental.pallas import tpu as pltpu
from jax.sharding import PartitionSpec as P

MESH = pl.DeviceIdType.MESH
F32 = jnp.float32
BF16 = jnp.bfloat16
I32 = jnp.int32
SLOTS = 16
SIDE = 4
LANES = 128
NT = (((1,), (1,)), ((), ()))
TN = (((0,), (0,)), ((), ()))
NN = (((1,), (0,)), ((), ()))


def iota(shape, axis):
    return lax.broadcasted_iota(I32, shape, axis)


def dot(a, b, dims=NN, precision=None):
    return lax.dot_general(a, b, dims, precision=precision, preferred_element_type=F32)


def exact(a, b, dims=NN):
    return dot(a, b, dims, lax.Precision.HIGHEST)


def thirds(v):
    a = v.astype(BF16).astype(F32)
    b = (v - a).astype(BF16).astype(F32)
    return a, b, v - a - b


def shift_of(n):
    return n.bit_length() - 1


def kernel(
    cot_hbm, act_hbm, logit_hbm, saved_hbm, w_hbm, rw_hbm, choice_hbm,
    hid_ref, tok_ref, rg_ref,
    cot_ref, act_ref, logit_ref, saved, rw_ref, choice_ref,
    cot_out, act_out, p_out, up, down, cot_own, cot_pair, act_own, p_own, p_pair,
    hot_own, hot_pair, xbuf, weights, acc, acc_out, part_core, part_chip,
    gate_one, gate_two, s_out, s_in, r_out, r_in, f_out, f_in,
    in_sem, w_sem, w_send, w_recv, saved_send, saved_recv,
    up_send, up_recv, near_send, hop_send, cot_recv, pair_send, pair_recv,
    act_send, act_recv, p_send, p_recv, p_two_send, p_two_recv, p_pair_send, p_pair_recv,
    x_send, x_one, x_two, core_send, core_recv, chip_send, chip_recv, one_send, one_recv, two_send, two_recv,
    s_send, s_recv, r_send, r_recv, f_send, f_recv,
):
    me, xy = lax.axis_index("expert"), lax.axis_index("tensor")
    groups = lax.axis_size("expert")
    chips = groups // 2
    experts, cap = choice_ref.shape
    own_tokens, feats = cot_ref.shape
    z, h = me // 2, me % 2
    e = z // 2
    x, y = xy // SIDE, xy % SIDE
    other_core = z * 2 + (1 - h)
    beside = x + 1 - 2 * (x % 2)
    beside_xy = beside * SIDE + y
    mirror_xy = (SIDE - 1 - x) * SIDE + y
    pair_z = z + 1 - 2 * (z % 2)
    pair = pair_z * 2 + h
    quarter = (z % 2) * 2 + h
    quarters = (other_core, pair, pair_z * 2 + (1 - h))
    far = 4
    token_shift, slot_shift = shift_of(own_tokens), shift_of(SLOTS)

    def remote(src, dst, send, recv, expert_at, tensor_at=xy):
        return pltpu.make_async_remote_copy(
            src_ref=src, dst_ref=dst, send_sem=send, recv_sem=recv,
            device_id=(expert_at, tensor_at), device_id_type=MESH,
        )

    def wait_bytes(ref, sem):
        pltpu.make_async_copy(ref, ref, sem).wait()

    waits = {}

    def later(name, ref, sem):
        waits[name] = lambda: wait_bytes(ref, sem)

    def finish(name):
        waits.pop(name)()

    def at_xy(i, j):
        return ((x + i) % SIDE) * SIDE + (y + j) % SIDE

    def at_z(k):
        return (z + 2 * k + 2 * chips) % chips

    arrays = {
        "choice": (choice_hbm, choice_ref), "cot": (cot_hbm, cot_ref), "act": (act_hbm, act_ref),
        "logit": (logit_hbm, logit_ref), "saved": (saved_hbm, saved.at[0]), "rw": (rw_hbm, rw_ref),
    }

    def load(*names):
        for name in names:
            src, dst = arrays[name]
            sem = in_sem.at[list(arrays).index(name)]
            pltpu.make_async_copy(src, dst, sem).start()
            later(name, dst, sem)

    load("choice", "cot")

    barrier = pltpu.get_barrier_semaphore()

    def greet(expert_at, tensor_at):
        pl.semaphore_signal(barrier, inc=1, device_id=(expert_at, tensor_at), device_id_type=MESH)

    near_steps = [k * sign for k in range(far, 0, -1) for sign in (1, -1)]
    for k in near_steps:
        for c in range(2):
            greet(at_z(k) * 2 + c, xy)
    for i in range(1, SIDE):
        greet(me, at_xy(0, i))
        greet(me, at_xy(i, 0))
        for q in quarters:
            greet(q, at_xy(i, 0))
    for q in quarters:
        greet(q, xy)
    greeted = 2 * len(near_steps) + 5 * (SIDE - 1) + len(quarters)

    finish("choice")
    tokens_at = iota((own_tokens, cap), 0) + me * own_tokens
    lane_expert = iota((own_tokens, LANES), 1)
    chosen = jnp.zeros((own_tokens, LANES), F32)
    for n in range(experts):
        hit = jnp.where(choice_ref[n : n + 1, :] == tokens_at, 1.0, 0.0)
        chosen = jnp.where(lane_expert == n, jnp.sum(hit, axis=1, keepdims=True), chosen)
    before = (iota((own_tokens, own_tokens), 1) < iota((own_tokens, own_tokens), 0)).astype(F32).astype(BF16)
    place = dot(before, chosen.astype(BF16))
    wide = experts * SLOTS
    group_of = (jnp.right_shift(iota((LANES, wide), 1), slot_shift) + e) & (experts - 1)
    spread = (group_of == iota((LANES, wide), 0)).astype(F32).astype(BF16)
    chosen_wide = dot(chosen.astype(BF16), spread)
    place_wide = dot(place.astype(BF16), spread)
    slot_lane = (iota((own_tokens, wide), 1) & (SLOTS - 1)).astype(F32)
    pick = jnp.where((chosen_wide > 0.5) & (place_wide == slot_lane), 1.0, 0.0)
    pick_bf = pick.astype(BF16)
    finish("cot")
    cot_slots = dot(pick_bf, cot_ref[...], TN).astype(BF16)
    cot_out[0] = cot_slots[:, :LANES].reshape(experts, SLOTS, LANES)
    cot_out[1] = cot_slots[:, LANES:].reshape(experts, SLOTS, LANES)

    pl.semaphore_wait(barrier, greeted)

    slots_of_core = pl.ds(pl.multiple_of(h * SLOTS, SLOTS), SLOTS)

    def relay_up(c, j):
        remote(
            cot_out.at[c, far + 1 + j], up.at[j, slots_of_core], up_send, up_recv.at[0, j], at_z(far) * 2 + c
        ).start()

    def relay_down(c, j):
        remote(
            cot_out.at[c, 2 * far + j], down.at[j, slots_of_core], up_send, up_recv.at[1, j], at_z(-far) * 2 + c
        ).start()

    relay_up(0, far - 1)
    relay_down(1, 0)
    for j in range(1, far):
        for c in range(2):
            relay_up(c, far - 1 - j)
            relay_down(c, j)
    pair_rows = 2 * SLOTS

    def rows_from(k):
        return pl.ds(pl.multiple_of(((e - k + experts) % experts) * pair_rows, pair_rows), pair_rows)

    mine = pl.ds(pl.multiple_of(e * pair_rows + h * SLOTS, SLOTS), SLOTS)
    for k in near_steps:
        for c in range(2):
            remote(
                cot_out.at[c, k % experts], cot_own.at[mine], near_send, cot_recv.at[k % experts], at_z(k) * 2 + c
            ).start()
    remote(cot_out.at[1 - h, 0], cot_own.at[mine], near_send, cot_recv.at[0], other_core).start()
    pltpu.make_async_copy(cot_out.at[h, 0], cot_own.at[mine], cot_recv.at[0]).start()
    later("near", cot_own.at[pl.ds(0, (2 * len(near_steps) + 1) * SLOTS)], near_send)

    def half_of(px, c, j):
        return w_hbm.at[:, pl.ds(pl.multiple_of((px * SIDE + j) * 2 * LANES + c * LANES, LANES), LANES)]

    load("act", "logit", "saved", "rw")
    for p, px in enumerate((x, SIDE - 1 - x)):
        for j in range(SIDE):
            pltpu.make_async_copy(half_of(px, h, j), weights.at[0, p * SIDE + j], w_sem).start()
    for p, px in enumerate((beside, SIDE - 1 - beside)):
        for j in range(SIDE):
            at = p * SIDE + j
            remote(half_of(px, h, j), weights.at[2, at], w_send, w_recv.at[1], me, beside_xy).start()
            remote(half_of(px, 1 - h, j), weights.at[3, at], w_send, w_recv.at[2], other_core, beside_xy).start()
    for p, px in enumerate((x, SIDE - 1 - x)):
        for j in range(SIDE):
            remote(half_of(px, 1 - h, j), weights.at[1, p * SIDE + j], w_send, w_recv.at[0], other_core).start()
    remote(saved_hbm, saved.at[2], saved_send, saved_recv.at[1], me, beside_xy).start()
    remote(saved_hbm, saved.at[1], saved_send, saved_recv.at[0], other_core).start()
    later("w0", weights.at[0], w_sem)
    later("w_send", weights.at[pl.ds(0, 3)], w_send)
    later("saved_send", saved.at[pl.ds(0, 3)], saved_send)
    for n in range(3):
        later(f"w{n + 1}", weights.at[n + 1], w_recv.at[n])
        later(f"saved{n + 1}", saved.at[n + 1], saved_recv.at[n])

    finish("act")
    act_slots = dot(pick_bf, act_ref[...], TN).astype(BF16)
    act_out[0] = act_slots[:, :LANES].reshape(experts, SLOTS, LANES)
    act_out[1] = act_slots[:, LANES:].reshape(experts, SLOTS, LANES)
    finish("logit")
    logits = logit_ref[...]
    grown = jnp.exp(logits - jnp.max(logits, axis=0, keepdims=True))
    probs = grown / jnp.sum(grown, axis=0, keepdims=True)
    lane = iota((experts, LANES), 1)
    copies = jnp.where((lane & (experts - 1)) == iota((experts, LANES), 0), 1.0, 0.0)
    p_terms = thirds(exact(probs, copies, TN))
    term = jnp.right_shift(iota((own_tokens, LANES), 1), shift_of(experts))
    p_wide = jnp.where(
        term == 0, p_terms[0], jnp.where(term == 1, p_terms[1], jnp.where(term == 2, p_terms[2], 0.0))
    )
    p_out[...] = dot(pick_bf, p_wide.astype(BF16), TN).astype(BF16).reshape(experts, SLOTS, LANES)

    middle = experts // 2

    def act_to(k):
        for c in range(2):
            remote(act_out.at[c, k], act_own.at[mine], act_send, act_recv, at_z(k) * 2 + c).start()

    def act_each(j, carry):
        act_to(middle - j)
        act_to(middle + j)
        return carry

    def p_to(k):
        for c in range(2):
            remote(p_out.at[k], p_own.at[mine], p_send, p_recv, at_z(k) * 2 + c).start()

    def send_rest():
        act_to(middle)
        lax.fori_loop(1, middle, act_each, 0)
        remote(act_out.at[1 - h, 0], act_own.at[mine], act_send, act_recv, other_core).start()
        pltpu.make_async_copy(act_out.at[h, 0], act_own.at[mine], act_recv).start()
        later("act_send", act_own.at[pl.ds(0, cap - SLOTS)], act_send)
        later("act_slots", act_own, act_recv)
        waits["p_send"] = p_sent

    def send_p():
        for m in range(SIDE - 1, 0, -1):
            p_to(m * SIDE + y)

        @pl.when(y != 0)
        def _():
            p_to(y)

        @pl.when(y == 0)
        def _():
            remote(p_out.at[0], p_own.at[mine], p_send, p_recv, other_core).start()
            pltpu.make_async_copy(p_out.at[0], p_own.at[mine], p_recv).start()

    def p_sent():
        sends = 2 * experts // SIDE

        @pl.when(y == 0)
        def _():
            wait_bytes(p_own.at[pl.ds(0, (sends - 1) * SLOTS)], p_send)

        @pl.when(y != 0)
        def _():
            wait_bytes(p_own.at[pl.ds(0, sends * SLOTS)], p_send)

    def share_p():
        wait_bytes(p_own.at[pl.ds(0, cap // SIDE)], p_recv)
        for m in range(SIDE):
            rows = rows_from(m * SIDE + y)
            for j in (2, 1, 3):
                remote(p_own.at[rows], p_own.at[rows], p_two_send, p_two_recv, me, at_xy(0, j)).start()
        rest = p_own.at[pl.ds(0, cap - cap // SIDE)]
        later("p_two_send", rest, p_two_send)
        later("p_slots", rest, p_two_recv)

    def share(k):
        rows = rows_from(k)
        wait_bytes(cot_own.at[rows], cot_recv.at[k % experts])
        remote(cot_own.at[rows], cot_pair.at[rows], pair_send, pair_recv, pair).start()

    later("pair_send", cot_pair, pair_send)
    later("pair", cot_pair, pair_recv)

    def hop_up(j):
        wait_bytes(up.at[j], up_recv.at[0, j])
        remote(
            up.at[j], cot_own.at[rows_from(far)], hop_send, cot_recv.at[far + 1 + j], at_z(1 + j) * 2 + h
        ).start()

    def hop_down(j):
        wait_bytes(down.at[j], up_recv.at[1, j])
        remote(
            down.at[j], cot_own.at[rows_from(-far)], hop_send, cot_recv.at[2 * far + j], at_z(j - far) * 2 + h
        ).start()

    for k in (0, 1, -1, 2, -2):
        share(k)
    @pl.when(h == 0)
    def _():
        hop_up(far - 1)

    @pl.when(h == 1)
    def _():
        hop_down(0)

    for j in range(1, far):
        hop_up(far - 1 - j)
        hop_down(j)
    relayed = cot_own.at[pl.ds(0, 2 * (2 * far - 1) * SLOTS)]
    send_p()
    later("up_send", relayed, up_send)
    later("hop_send", relayed, hop_send)

    wanted = choice_ref[pl.ds(e, 1), :].astype(F32)
    wanted_col = jnp.transpose(jnp.broadcast_to(wanted, (LANES, cap)))[:, :1].astype(I32)
    wanted_row = wanted.astype(I32)
    owner_col = jnp.right_shift(wanted_col, token_shift)
    owner_row = jnp.right_shift(wanted_row, token_shift)
    earlier = (owner_row == owner_col) & (wanted_row < wanted_col)
    rank = jnp.sum(jnp.where(earlier, 1.0, 0.0), axis=1, keepdims=True).astype(I32)
    slot = jnp.right_shift(owner_col, 2) * pair_rows + (owner_col & 1) * SLOTS + rank
    ours = (jnp.right_shift(owner_col, 1) & 1) == z % 2
    slot_lanes = iota((cap, cap), 1)
    hot_own[...] = jnp.where(jnp.where(ours, slot, -1) == slot_lanes, 1.0, 0.0).astype(BF16)
    hot_pair[...] = jnp.where(jnp.where(ours, -1, slot) == slot_lanes, 1.0, 0.0).astype(BF16)

    for k in (3, -3, 4, -4, 5, -5, 6, -6, 7, -7, 8):
        share(k)
    half = cap // 2
    picked = dot(hot_own[...], cot_own[...])
    finish("pair")

    order = (1, 3, 2)

    def rows_of(first):
        return pl.ds(first * half, half)

    def send_block(first, src, dst, recv, to):
        remote(xbuf.at[src, rows_of(first)], xbuf.at[dst, rows_of(first)], x_send, recv, me, to).start()

    def from_y(j):
        return (y - j + SIDE) % SIDE

    for first in range(2):
        rows = slice(first * half, (first + 1) * half)
        xbuf[y, rows_of(first), :] = (picked[rows] + dot(hot_pair[rows, :], cot_pair[...])).astype(BF16)
        if first == 0:
            send_block(0, y, SIDE + y, x_one.at[0, 0], mirror_xy)
        else:
            for j in order:
                send_block(1, y, y, x_one.at[1, j], at_xy(0, j))
    for j in order:
        send_block(0, y, y, x_two.at[0, 0, j], at_xy(0, j))
    send_block(1, y, SIDE + y, x_two.at[1, 0, 0], mirror_xy)
    later("x_send", xbuf.at[pl.ds(0, 2 * SIDE - 1)], x_send)
    send_rest()
    wait_bytes(xbuf.at[SIDE + y, rows_of(0)], x_one.at[0, 0])
    for j in order:
        send_block(0, SIDE + y, SIDE + y, x_two.at[0, 1, j], at_xy(0, j))
    for j in order:
        wait_bytes(xbuf.at[from_y(j), rows_of(1)], x_one.at[1, j])
        send_block(1, from_y(j), SIDE + from_y(j), x_two.at[1, 0, j], mirror_xy)
    share_p()
    finish("saved2")
    remote(saved.at[2], saved.at[3], saved_send, saved_recv.at[2], other_core).start()
    for n in range(4):
        finish(f"w{n}")

    def product(p, first, n):
        blocks_at = range(p * SIDE, (p + 1) * SIDE)
        lhs = jnp.concatenate([xbuf[b, first * half : (first + 1) * half, :] for b in blocks_at], axis=1)
        rhs = jnp.concatenate([weights[n, b] for b in blocks_at], axis=1)
        return dot(lhs, rhs, NT)

    def span(first):
        return slice(first * half, (first + 1) * half)

    for j in order:
        wait_bytes(xbuf.at[from_y(j), rows_of(0)], x_two.at[0, 0, j])
    for first in range(2):
        for n in range(4):
            acc[n, span(first), :] = product(0, first, n)
    for first in range(2):
        for j in order if first == 0 else (0, *order):
            sem = x_two.at[0, 1, j] if first == 0 else x_two.at[1, 0, j]
            wait_bytes(xbuf.at[SIDE + from_y(j), rows_of(first)], sem)
        for n in range(4):
            acc[n, span(first), :] += product(1, first, n)

    finish("saved")
    finish("saved1")
    finish("saved3")
    prod = sum(saved[n].astype(F32) * acc[n] for n in range(4))
    gate = jnp.sum(jnp.transpose(prod[:, :LANES] + prod[:, LANES:]), axis=0, keepdims=True)
    pieces = cap // LANES
    slot_one = x * 4 + quarter
    for k in range(pieces):
        gate_one[slot_one, k : k + 1, :] = gate[0:1, k * LANES : (k + 1) * LANES]
    for i in (2, 1, 3, 0):
        for q in quarters + (() if i == 0 else (me,)):
            remote(gate_one.at[slot_one], gate_one.at[slot_one], one_send, one_recv, q, at_xy(i, 0)).start()
    later("one_send", gate_one.at[pl.ds(0, 4 * SIDE - 1)], one_send)
    wait_bytes(gate_one.at[pl.ds(0, 4 * SIDE - 1)], one_recv)
    gate_two[y] = jnp.sum(gate_one[...], axis=0)
    for j in (2, 1, 3):
        remote(gate_two.at[y], gate_two.at[y], two_send, two_recv, me, at_xy(0, j)).start()
    later("two_send", gate_two.at[pl.ds(0, SIDE - 1)], two_send)

    remote(acc.at[1], part_core, core_send, core_recv, other_core).start()
    for n, to in enumerate((me, other_core)):
        acc_out[n] = acc[2 + n].astype(BF16)
        remote(acc_out.at[n], part_chip.at[n], chip_send.at[n], chip_recv.at[n], to, beside_xy).start()
        later(f"chip_send{n}", part_chip.at[n], chip_send.at[n])
        later(f"part{n}", part_chip.at[n], chip_recv.at[n])
    later("core_send", part_core, core_send)
    later("part", part_core, core_recv)

    finish("p_slots")
    p_to_pair = remote(p_own, p_pair, p_pair_send, p_pair_recv, pair)
    p_to_pair.start()
    later("p_pair_send", p_pair, p_pair_send)
    later("p_pair", p_pair, p_pair_recv)
    select = jnp.where(lane < 3 * experts, copies, 0.0)
    p_slot = dot(select.astype(BF16), p_own[...], NT)
    mine_row = iota((experts, cap), 0) == e
    p_mine = jnp.sum(jnp.where(mine_row, p_slot, 0.0), axis=0, keepdims=True)
    slope = p_mine * (jnp.where(mine_row, 1.0, 0.0) - p_slot)
    slope_row = dot(jnp.concatenate(thirds(slope), axis=0).astype(BF16), hot_own[...], NT)
    slope_row = slope_row[:experts] + slope_row[experts : 2 * experts] + slope_row[2 * experts :]
    finish("act_slots")
    act_row = dot(hot_own[...], act_own[...]).astype(BF16)

    wait_bytes(gate_two.at[pl.ds(0, SIDE - 1)], two_recv)
    total = jnp.sum(gate_two[...], axis=0)
    total_row = jnp.concatenate([total[k : k + 1, :] for k in range(pieces)], axis=1)

    def back(name, out, into, send, recv):
        def one(k):
            to = (z + 2 * k) % chips
            remote(out(to // 2), into.at[e], send, recv, to * 2 + h).start()

        middle = experts // 2
        one(middle)

        def each(j, carry):
            one(middle - j)
            one(middle + j)
            return carry

        lax.fori_loop(1, middle, each, 0)
        later(name + "_send", into.at[pl.ds(0, experts - 1)], send)
        later(name, into.at[pl.ds(0, experts - 1)], recv)

    w_row = total_row * slope_row
    r_three = dot(jnp.concatenate(thirds(w_row), axis=0).astype(BF16), act_row)
    r_part = r_three[:experts] + r_three[experts : 2 * experts] + r_three[2 * experts :]
    r_out[...] = r_part.astype(BF16)
    back("r", lambda k: r_out, r_in, r_send, r_recv)
    rows3 = jnp.concatenate([total_row, jnp.zeros((7, cap), F32)], axis=0)
    s_three = dot(jnp.concatenate(thirds(rows3), axis=0).astype(BF16), hot_own[...])
    s_slot = s_three[0:1] + s_three[8:9] + s_three[16:17]
    slot_at = iota((experts, cap), 1)
    of_owner = (jnp.right_shift(slot_at, slot_shift + 1) == iota((experts, cap), 0)) & (
        (jnp.right_shift(slot_at, slot_shift) & 1) == h
    )
    fold = jnp.where((iota((cap, LANES), 0) & (SLOTS - 1)) == iota((cap, LANES), 1), 1.0, 0.0)
    s_spread = jnp.concatenate(thirds(jnp.where(of_owner, s_slot, 0.0)), axis=0).astype(BF16)
    s_three = dot(s_spread, fold.astype(BF16))
    s_rows = s_three[:experts] + s_three[experts : 2 * experts] + s_three[2 * experts :]
    for k in range(experts):
        s_out[k] = s_rows[k : k + 1, :]

    back("s", lambda k: s_out.at[k], s_in, s_send, s_recv)
    r_in[e] = r_out[...]
    s_in[e] = s_out[e]

    finish("p_pair")
    gates = dot(hot_own[...], p_own[...]) + dot(hot_pair[...], p_pair[...])
    gate_col = jnp.sum(jnp.where(iota((cap, LANES), 1) == e, gates, 0.0), axis=1, keepdims=True)
    finish("part")
    finish("part0")
    finish("part1")
    pre = acc[0] + part_core[...] + (part_chip[0].astype(F32) + part_chip[1].astype(F32))
    hid_ref[...] = (gate_col * pre).astype(BF16)

    finish("rw")
    finish("s")
    s_all = jnp.concatenate([s_in[k] for k in range(experts)], axis=0)
    unfold = jnp.where((iota((LANES, wide), 1) & (SLOTS - 1)) == iota((LANES, wide), 0), 1.0, 0.0)
    s_three = dot(jnp.concatenate(thirds(s_all), axis=0).astype(BF16), unfold.astype(BF16))
    s_sum = s_three[:experts] + s_three[experts : 2 * experts] + s_three[2 * experts :]
    own_lane = ((jnp.right_shift(iota((experts, wide), 1), slot_shift) + e) & (experts - 1)) == iota((experts, wide), 0)
    score3 = dot(jnp.concatenate(thirds(jnp.where(own_lane, s_sum, 0.0)), axis=0).astype(BF16), pick_bf, NT)
    score = score3[:experts] + score3[experts : 2 * experts] + score3[2 * experts :]
    inner = jnp.sum(probs * score, axis=0, keepdims=True)
    logit_grad = (probs * (score - inner)).astype(BF16)
    tok_ref[...] = dot(logit_grad, rw_ref[...], TN).astype(BF16)

    finish("r")
    f_out[...] = jnp.sum(r_in[...].astype(F32), axis=0)
    f_in[quarter] = f_out[...]
    for q in quarters:
        remote(f_out, f_in.at[quarter], f_send, f_recv, q).start()
    later("f_send", f_in.at[pl.ds(0, len(quarters))], f_send)
    wait_bytes(f_in.at[pl.ds(0, len(quarters))], f_recv)
    rg_ref[:, :LANES] = f_in[0] + f_in[2]
    rg_ref[:, LANES:] = f_in[1] + f_in[3]

    for name in list(waits):
        finish(name)


def write(hid_ref, tok_ref, rg_ref, hid_out, tok_out, rg_out, sem):
    copies = [
        pltpu.make_async_copy(src, dst, sem.at[n])
        for n, (src, dst) in enumerate(((hid_ref, hid_out), (tok_ref, tok_out), (rg_ref, rg_out)))
    ]
    for copy in copies:
        copy.start()
    for copy in copies:
        copy.wait()


def on_device(
    cotangent, activations, router_logits, saved_hidden, down_weight, router_weight, choices
):
    experts, cap = choices.shape
    own_tokens, feats = cotangent.shape
    hidden = down_weight.shape[0]
    wide = experts * SLOTS
    blocks = SIDE * SIDE
    vmem = pl.BlockSpec(memory_space=pltpu.VMEM)
    hbm = pl.BlockSpec(memory_space=pltpu.HBM)
    dma = pltpu.SemaphoreType.DMA
    shapes = (
        jax.ShapeDtypeStruct((cap, hidden), BF16),
        jax.ShapeDtypeStruct((own_tokens, feats), BF16),
        jax.ShapeDtypeStruct((experts, feats), F32),
    )
    grads = pl.pallas_call(
        kernel,
        out_shape=shapes,
        in_specs=[hbm] * 7,
        out_specs=(vmem, vmem, vmem),
        scratch_shapes=[
            pltpu.VMEM((own_tokens, feats), BF16),
            pltpu.VMEM((own_tokens, feats), BF16),
            pltpu.VMEM((experts, own_tokens), F32),
            pltpu.VMEM((4, cap, hidden), BF16),
            pltpu.VMEM((experts, feats), BF16),
            pltpu.VMEM((experts, cap), I32),
            pltpu.VMEM((2, experts, SLOTS, LANES), BF16),
            pltpu.VMEM((2, experts, SLOTS, LANES), BF16),
            pltpu.VMEM((experts, SLOTS, LANES), BF16),
            pltpu.VMEM((4, 2 * SLOTS, LANES), BF16),
            pltpu.VMEM((4, 2 * SLOTS, LANES), BF16),
            pltpu.VMEM((cap, LANES), BF16),
            pltpu.VMEM((cap, LANES), BF16),
            pltpu.VMEM((cap, LANES), BF16),
            pltpu.VMEM((cap, LANES), BF16),
            pltpu.VMEM((cap, LANES), BF16),
            pltpu.VMEM((cap, cap), BF16),
            pltpu.VMEM((cap, cap), BF16),
            pltpu.VMEM((2 * SIDE, cap, LANES), BF16),
            pltpu.VMEM((4, 2 * SIDE, hidden, LANES), BF16),
            pltpu.VMEM((4, cap, hidden), F32),
            pltpu.VMEM((2, cap, hidden), BF16),
            pltpu.VMEM((cap, hidden), F32),
            pltpu.VMEM((2, cap, hidden), BF16),
            pltpu.VMEM((4 * SIDE, cap // LANES, LANES), F32),
            pltpu.VMEM((SIDE, cap // LANES, LANES), F32),
            pltpu.VMEM((experts, 1, LANES), F32),
            pltpu.VMEM((experts, 1, LANES), F32),
            pltpu.VMEM((experts, LANES), BF16),
            pltpu.VMEM((experts, experts, LANES), BF16),
            pltpu.VMEM((experts, LANES), F32),
            pltpu.VMEM((4, experts, LANES), F32),
            dma((6,)), dma(()), dma(()), dma((3,)), dma(()), dma((3,)),
            dma(()), dma((2, 4)), dma(()), dma(()), dma((experts,)), dma(()), dma(()),
            dma(()), dma(()), dma(()), dma(()), dma(()), dma(()), dma(()), dma(()),
            dma(()), dma((2, SIDE)), dma((2, 2, SIDE)), dma(()), dma(()), dma((2,)), dma((2,)),
            dma(()), dma(()), dma(()), dma(()),
            dma(()), dma(()), dma(()), dma(()), dma(()), dma(()),
        ],
        compiler_params=pltpu.CompilerParams(
            collective_id=0, has_side_effects=True, vmem_limit_bytes=48 * 2**20
        ),
        cost_estimate=pl.CostEstimate(
            flops=2 * cap * hidden * feats * blocks, bytes_accessed=4 * 2**20, transcendentals=0
        ),
        name="gated_moe_backward",
    )(
        *(
            pltpu.with_memory_space_constraint(v, pltpu.HBM)
            for v in (
                cotangent, activations, router_logits.T, saved_hidden, down_weight, router_weight.T, choices
            )
        )
    )
    hidden_grad, token_grad, router_grad = pl.pallas_call(
        write,
        out_shape=shapes,
        in_specs=[vmem] * 3,
        out_specs=(hbm, hbm, hbm),
        scratch_shapes=[dma((3,))],
        compiler_params=pltpu.CompilerParams(vmem_limit_bytes=2 * 2**20),
        name="write_gradients",
    )(*grads)
    return hidden_grad, token_grad, router_grad.T


def solution(mesh):
    placed = (
        P("expert", "tensor"),
        P("expert", "tensor"),
        P("expert", None),
        P(None, ("expert", "tensor")),
        P(("expert", "tensor"), None),
        P("tensor", None),
        P(),
    )
    return jax.shard_map(
        on_device,
        mesh=mesh,
        in_specs=placed,
        out_specs=(P(None, ("expert", "tensor")), P("expert", "tensor"), P("tensor", None)),
        check_vma=False,
    )
```

```python
import functools

import jax
import jax.numpy as jnp
from jax import lax
from jax.experimental import pallas as pl
from jax.experimental.pallas import tpu as pltpu
from jax.sharding import PartitionSpec as P

MESH = pl.DeviceIdType.MESH
F32 = jnp.float32
BF16 = jnp.bfloat16
I32 = jnp.int32
SLOTS = 16
SIDE = 4
LANES = 128
NT = (((1,), (1,)), ((), ()))
TN = (((0,), (0,)), ((), ()))
NN = (((1,), (0,)), ((), ()))


def iota(shape, axis):
    return lax.broadcasted_iota(I32, shape, axis)


def dot(a, b, dims=NN, precision=None):
    return lax.dot_general(a, b, dims, precision=precision, preferred_element_type=F32)


def exact(a, b, dims=NN):
    return dot(a, b, dims, lax.Precision.HIGHEST)


def thirds(v):
    a = v.astype(BF16).astype(F32)
    b = (v - a).astype(BF16).astype(F32)
    return a, b, v - a - b


def shift_of(n):
    return n.bit_length() - 1


def kernel(
    cot_hbm, act_hbm, logit_hbm, saved_hbm, w_hbm, rw_hbm, choice_hbm,
    hid_ref, tok_ref, rg_ref,
    cot_ref, act_ref, logit_ref, saved, rw_ref, choice_ref,
    cot_out, act_out, p_out, up, down, cot_own, cot_pair, act_own, p_own, p_pair,
    hot_own, hot_pair, xbuf, weights, acc, acc_out, part_core, part_chip,
    gate_one, gate_two, s_out, s_in, r_out, r_mid, r_in, f_out, f_in,
    in_sem, w_sem, w_send, w_recv, saved_send, saved_recv,
    up_send, up_recv, near_send, hop_send, cot_recv, pair_send, pair_recv,
    act_send, act_recv, p_send, p_recv, p_two_send, p_two_recv, p_pair_send, p_pair_recv,
    x_send, x_one, x_two, core_send, core_recv, chip_send, chip_recv, one_send, one_recv, two_send, two_recv,
    s_send, s_recv, r_send, r_mid_send, r_recv, f_send, f_recv,
):
    me, xy = lax.axis_index("expert"), lax.axis_index("tensor")
    groups = lax.axis_size("expert")
    chips = groups // 2
    experts, cap = choice_ref.shape
    own_tokens, feats = cot_ref.shape
    z, h = me // 2, me % 2
    e = z // 2
    x, y = xy // SIDE, xy % SIDE
    other_core = z * 2 + (1 - h)
    beside = x + 1 - 2 * (x % 2)
    beside_xy = beside * SIDE + y
    mirror_xy = (SIDE - 1 - x) * SIDE + y
    pair_z = z + 1 - 2 * (z % 2)
    pair = pair_z * 2 + h
    quarter = (z % 2) * 2 + h
    quarters = (other_core, pair, pair_z * 2 + (1 - h))
    far = 4
    token_shift, slot_shift = shift_of(own_tokens), shift_of(SLOTS)

    def remote(src, dst, send, recv, expert_at, tensor_at=xy):
        return pltpu.make_async_remote_copy(
            src_ref=src, dst_ref=dst, send_sem=send, recv_sem=recv,
            device_id=(expert_at, tensor_at), device_id_type=MESH,
        )

    def wait_bytes(ref, sem):
        pltpu.make_async_copy(ref, ref, sem).wait()

    waits = {}

    def later(name, ref, sem):
        waits[name] = lambda: wait_bytes(ref, sem)

    def finish(name):
        waits.pop(name)()

    def at_xy(i, j):
        return ((x + i) % SIDE) * SIDE + (y + j) % SIDE

    def at_z(k):
        return (z + 2 * k + 2 * chips) % chips

    arrays = {
        "choice": (choice_hbm, choice_ref), "cot": (cot_hbm, cot_ref), "act": (act_hbm, act_ref),
        "logit": (logit_hbm, logit_ref), "saved": (saved_hbm, saved.at[0]), "rw": (rw_hbm, rw_ref),
    }

    def load(*names):
        for name in names:
            src, dst = arrays[name]
            sem = in_sem.at[list(arrays).index(name)]
            pltpu.make_async_copy(src, dst, sem).start()
            later(name, dst, sem)

    load("choice", "cot")

    barrier = pltpu.get_barrier_semaphore()

    def greet(expert_at, tensor_at):
        pl.semaphore_signal(barrier, inc=1, device_id=(expert_at, tensor_at), device_id_type=MESH)

    near_steps = [k * sign for k in range(far, 0, -1) for sign in (1, -1)]
    for k in near_steps:
        for c in range(2):
            greet(at_z(k) * 2 + c, xy)
    for i in range(1, SIDE):
        greet(me, at_xy(0, i))
        greet(me, at_xy(i, 0))
        for q in quarters:
            greet(q, at_xy(i, 0))
    for q in quarters:
        greet(q, xy)
    greeted = 2 * len(near_steps) + 5 * (SIDE - 1) + len(quarters)

    finish("choice")
    tokens_at = iota((own_tokens, cap), 0) + me * own_tokens
    lane_expert = iota((own_tokens, LANES), 1)
    chosen = jnp.zeros((own_tokens, LANES), F32)
    for n in range(experts):
        hit = jnp.where(choice_ref[n : n + 1, :] == tokens_at, 1.0, 0.0)
        chosen = jnp.where(lane_expert == n, jnp.sum(hit, axis=1, keepdims=True), chosen)
    before = (iota((own_tokens, own_tokens), 1) < iota((own_tokens, own_tokens), 0)).astype(F32).astype(BF16)
    place = dot(before, chosen.astype(BF16))
    wide = experts * SLOTS
    group_of = (jnp.right_shift(iota((LANES, wide), 1), slot_shift) + e) & (experts - 1)
    spread = (group_of == iota((LANES, wide), 0)).astype(F32).astype(BF16)
    chosen_wide = dot(chosen.astype(BF16), spread)
    place_wide = dot(place.astype(BF16), spread)
    slot_lane = (iota((own_tokens, wide), 1) & (SLOTS - 1)).astype(F32)
    pick = jnp.where((chosen_wide > 0.5) & (place_wide == slot_lane), 1.0, 0.0)
    pick_bf = pick.astype(BF16)
    finish("cot")
    cot_slots = dot(pick_bf, cot_ref[...], TN).astype(BF16)
    cot_out[0] = cot_slots[:, :LANES].reshape(experts, SLOTS, LANES)
    cot_out[1] = cot_slots[:, LANES:].reshape(experts, SLOTS, LANES)

    pl.semaphore_wait(barrier, greeted)

    slots_of_core = pl.ds(pl.multiple_of(h * SLOTS, SLOTS), SLOTS)

    def relay_up(c, j):
        remote(
            cot_out.at[c, far + 1 + j], up.at[j, slots_of_core], up_send, up_recv.at[0, j], at_z(far) * 2 + c
        ).start()

    def relay_down(c, j):
        remote(
            cot_out.at[c, 2 * far + j], down.at[j, slots_of_core], up_send, up_recv.at[1, j], at_z(-far) * 2 + c
        ).start()

    relay_up(0, far - 1)
    relay_down(1, 0)
    for j in range(1, far):
        for c in range(2):
            relay_up(c, far - 1 - j)
            relay_down(c, j)
    pair_rows = 2 * SLOTS

    def rows_from(k):
        return pl.ds(pl.multiple_of(((e - k + experts) % experts) * pair_rows, pair_rows), pair_rows)

    mine = pl.ds(pl.multiple_of(e * pair_rows + h * SLOTS, SLOTS), SLOTS)
    for k in near_steps:
        for c in range(2):
            remote(
                cot_out.at[c, k % experts], cot_own.at[mine], near_send, cot_recv.at[k % experts], at_z(k) * 2 + c
            ).start()
    remote(cot_out.at[1 - h, 0], cot_own.at[mine], near_send, cot_recv.at[0], other_core).start()
    pltpu.make_async_copy(cot_out.at[h, 0], cot_own.at[mine], cot_recv.at[0]).start()
    later("near", cot_own.at[pl.ds(0, (2 * len(near_steps) + 1) * SLOTS)], near_send)

    def half_of(px, c, j):
        return w_hbm.at[:, pl.ds(pl.multiple_of((px * SIDE + j) * 2 * LANES + c * LANES, LANES), LANES)]

    load("act", "logit", "saved", "rw")
    for p, px in enumerate((x, SIDE - 1 - x)):
        for j in range(SIDE):
            pltpu.make_async_copy(half_of(px, h, j), weights.at[0, p * SIDE + j], w_sem).start()
    for p, px in enumerate((beside, SIDE - 1 - beside)):
        for j in range(SIDE):
            at = p * SIDE + j
            remote(half_of(px, h, j), weights.at[2, at], w_send, w_recv.at[1], me, beside_xy).start()
            remote(half_of(px, 1 - h, j), weights.at[3, at], w_send, w_recv.at[2], other_core, beside_xy).start()
    for p, px in enumerate((x, SIDE - 1 - x)):
        for j in range(SIDE):
            remote(half_of(px, 1 - h, j), weights.at[1, p * SIDE + j], w_send, w_recv.at[0], other_core).start()
    remote(saved_hbm, saved.at[2], saved_send, saved_recv.at[1], me, beside_xy).start()
    remote(saved_hbm, saved.at[1], saved_send, saved_recv.at[0], other_core).start()
    later("w0", weights.at[0], w_sem)
    later("w_send", weights.at[pl.ds(0, 3)], w_send)
    later("saved_send", saved.at[pl.ds(0, 3)], saved_send)
    for n in range(3):
        later(f"w{n + 1}", weights.at[n + 1], w_recv.at[n])
        later(f"saved{n + 1}", saved.at[n + 1], saved_recv.at[n])

    finish("act")
    act_slots = dot(pick_bf, act_ref[...], TN).astype(BF16)
    act_out[0] = act_slots[:, :LANES].reshape(experts, SLOTS, LANES)
    act_out[1] = act_slots[:, LANES:].reshape(experts, SLOTS, LANES)
    finish("logit")
    logits = logit_ref[...]
    grown = jnp.exp(logits - jnp.max(logits, axis=0, keepdims=True))
    probs = grown / jnp.sum(grown, axis=0, keepdims=True)
    lane = iota((experts, LANES), 1)
    copies = jnp.where((lane & (experts - 1)) == iota((experts, LANES), 0), 1.0, 0.0)
    p_terms = thirds(exact(probs, copies, TN))
    term = jnp.right_shift(iota((own_tokens, LANES), 1), shift_of(experts))
    p_wide = jnp.where(
        term == 0, p_terms[0], jnp.where(term == 1, p_terms[1], jnp.where(term == 2, p_terms[2], 0.0))
    )
    p_out[...] = dot(pick_bf, p_wide.astype(BF16), TN).astype(BF16).reshape(experts, SLOTS, LANES)

    middle = experts // 2

    def act_to(k):
        for c in range(2):
            remote(act_out.at[c, k], act_own.at[mine], act_send, act_recv, at_z(k) * 2 + c).start()

    def act_each(j, carry):
        act_to(middle - j)
        act_to(middle + j)
        return carry

    def p_to(k):
        for c in range(2):
            remote(p_out.at[k], p_own.at[mine], p_send, p_recv, at_z(k) * 2 + c).start()

    def send_rest():
        act_to(middle)
        lax.fori_loop(1, middle, act_each, 0)
        remote(act_out.at[1 - h, 0], act_own.at[mine], act_send, act_recv, other_core).start()
        pltpu.make_async_copy(act_out.at[h, 0], act_own.at[mine], act_recv).start()
        later("act_send", act_own.at[pl.ds(0, cap - SLOTS)], act_send)
        later("act_slots", act_own, act_recv)
        waits["p_send"] = p_sent

    def send_p():
        for m in range(SIDE - 1, 0, -1):
            p_to(m * SIDE + y)

        @pl.when(y != 0)
        def _():
            p_to(y)

        @pl.when(y == 0)
        def _():
            remote(p_out.at[0], p_own.at[mine], p_send, p_recv, other_core).start()
            pltpu.make_async_copy(p_out.at[0], p_own.at[mine], p_recv).start()

    def p_sent():
        sends = 2 * experts // SIDE

        @pl.when(y == 0)
        def _():
            wait_bytes(p_own.at[pl.ds(0, (sends - 1) * SLOTS)], p_send)

        @pl.when(y != 0)
        def _():
            wait_bytes(p_own.at[pl.ds(0, sends * SLOTS)], p_send)

    def share_p():
        wait_bytes(p_own.at[pl.ds(0, cap // SIDE)], p_recv)
        for m in range(SIDE):
            rows = rows_from(m * SIDE + y)
            for j in (2, 1, 3):
                remote(p_own.at[rows], p_own.at[rows], p_two_send, p_two_recv, me, at_xy(0, j)).start()
        rest = p_own.at[pl.ds(0, cap - cap // SIDE)]
        later("p_two_send", rest, p_two_send)
        later("p_slots", rest, p_two_recv)

    def share(k):
        rows = rows_from(k)
        wait_bytes(cot_own.at[rows], cot_recv.at[k % experts])
        remote(cot_own.at[rows], cot_pair.at[rows], pair_send, pair_recv, pair).start()

    later("pair_send", cot_pair, pair_send)
    later("pair", cot_pair, pair_recv)

    def hop_up(j):
        wait_bytes(up.at[j], up_recv.at[0, j])
        remote(
            up.at[j], cot_own.at[rows_from(far)], hop_send, cot_recv.at[far + 1 + j], at_z(1 + j) * 2 + h
        ).start()

    def hop_down(j):
        wait_bytes(down.at[j], up_recv.at[1, j])
        remote(
            down.at[j], cot_own.at[rows_from(-far)], hop_send, cot_recv.at[2 * far + j], at_z(j - far) * 2 + h
        ).start()

    for k in (0, 1, -1, 2, -2):
        share(k)
    @pl.when(h == 0)
    def _():
        hop_up(far - 1)

    @pl.when(h == 1)
    def _():
        hop_down(0)

    for j in range(1, far):
        hop_up(far - 1 - j)
        hop_down(j)
    relayed = cot_own.at[pl.ds(0, 2 * (2 * far - 1) * SLOTS)]
    send_p()
    later("up_send", relayed, up_send)
    later("hop_send", relayed, hop_send)

    wanted = choice_ref[pl.ds(e, 1), :].astype(F32)
    wanted_col = jnp.transpose(jnp.broadcast_to(wanted, (LANES, cap)))[:, :1].astype(I32)
    wanted_row = wanted.astype(I32)
    owner_col = jnp.right_shift(wanted_col, token_shift)
    owner_row = jnp.right_shift(wanted_row, token_shift)
    earlier = (owner_row == owner_col) & (wanted_row < wanted_col)
    rank = jnp.sum(jnp.where(earlier, 1.0, 0.0), axis=1, keepdims=True).astype(I32)
    slot = jnp.right_shift(owner_col, 2) * pair_rows + (owner_col & 1) * SLOTS + rank
    ours = (jnp.right_shift(owner_col, 1) & 1) == z % 2
    slot_lanes = iota((cap, cap), 1)
    hot_own[...] = jnp.where(jnp.where(ours, slot, -1) == slot_lanes, 1.0, 0.0).astype(BF16)
    hot_pair[...] = jnp.where(jnp.where(ours, -1, slot) == slot_lanes, 1.0, 0.0).astype(BF16)

    for k in (3, -3, 4, -4, 5, -5, 6, -6, 7, -7, 8):
        share(k)
    half = cap // 2
    picked = dot(hot_own[...], cot_own[...])
    finish("pair")

    order = (1, 3, 2)

    def rows_of(first):
        return pl.ds(first * half, half)

    def send_block(first, src, dst, recv, to):
        remote(xbuf.at[src, rows_of(first)], xbuf.at[dst, rows_of(first)], x_send, recv, me, to).start()

    def from_y(j):
        return (y - j + SIDE) % SIDE

    for first in range(2):
        rows = slice(first * half, (first + 1) * half)
        xbuf[y, rows_of(first), :] = (picked[rows] + dot(hot_pair[rows, :], cot_pair[...])).astype(BF16)
        if first == 0:
            send_block(0, y, SIDE + y, x_one.at[0, 0], mirror_xy)
        else:
            for j in order:
                send_block(1, y, y, x_one.at[1, j], at_xy(0, j))
    for j in order:
        send_block(0, y, y, x_two.at[0, 0, j], at_xy(0, j))
    send_block(1, y, SIDE + y, x_two.at[1, 0, 0], mirror_xy)
    later("x_send", xbuf.at[pl.ds(0, 2 * SIDE - 1)], x_send)
    send_rest()
    wait_bytes(xbuf.at[SIDE + y, rows_of(0)], x_one.at[0, 0])
    for j in order:
        send_block(0, SIDE + y, SIDE + y, x_two.at[0, 1, j], at_xy(0, j))
    for j in order:
        wait_bytes(xbuf.at[from_y(j), rows_of(1)], x_one.at[1, j])
        send_block(1, from_y(j), SIDE + from_y(j), x_two.at[1, 0, j], mirror_xy)
    share_p()
    finish("saved2")
    remote(saved.at[2], saved.at[3], saved_send, saved_recv.at[2], other_core).start()
    for n in range(4):
        finish(f"w{n}")

    def product(p, first, n):
        blocks_at = range(p * SIDE, (p + 1) * SIDE)
        lhs = jnp.concatenate([xbuf[b, first * half : (first + 1) * half, :] for b in blocks_at], axis=1)
        rhs = jnp.concatenate([weights[n, b] for b in blocks_at], axis=1)
        return dot(lhs, rhs, NT)

    def span(first):
        return slice(first * half, (first + 1) * half)

    for j in order:
        wait_bytes(xbuf.at[from_y(j), rows_of(0)], x_two.at[0, 0, j])
    for first in range(2):
        for n in range(4):
            acc[n, span(first), :] = product(0, first, n)
    finish("saved")
    finish("saved1")
    finish("saved3")
    slot_one = x * 4 + quarter
    pieces = half // LANES
    for first in range(2):
        for j in order if first == 0 else (0, *order):
            sem = x_two.at[0, 1, j] if first == 0 else x_two.at[1, 0, j]
            wait_bytes(xbuf.at[SIDE + from_y(j), rows_of(first)], sem)
        prod = 0.0
        for n in range(4):
            pre = acc[n, span(first), :] + product(1, first, n)
            acc[n, span(first), :] = pre
            prod += saved[n, span(first), :].astype(F32) * pre
        gate = jnp.sum(jnp.transpose(prod[:, :LANES] + prod[:, LANES:]), axis=0, keepdims=True)
        for k in range(pieces):
            gate_one[slot_one, first * pieces + k : first * pieces + k + 1, :] = gate[:, k * LANES : (k + 1) * LANES]

    for i in (2, 1, 3, 0):
        for q in quarters + (() if i == 0 else (me,)):
            remote(gate_one.at[slot_one], gate_one.at[slot_one], one_send, one_recv, q, at_xy(i, 0)).start()
    later("one_send", gate_one.at[pl.ds(0, 4 * SIDE - 1)], one_send)
    wait_bytes(gate_one.at[pl.ds(0, 4 * SIDE - 1)], one_recv)
    gate_two[y] = jnp.sum(gate_one[...], axis=0)
    for j in (2, 1, 3):
        remote(gate_two.at[y], gate_two.at[y], two_send, two_recv, me, at_xy(0, j)).start()
    later("two_send", gate_two.at[pl.ds(0, SIDE - 1)], two_send)

    remote(acc.at[1], part_core, core_send, core_recv, other_core).start()
    for n, to in enumerate((me, other_core)):
        acc_out[n] = acc[2 + n].astype(BF16)
        remote(acc_out.at[n], part_chip.at[n], chip_send.at[n], chip_recv.at[n], to, beside_xy).start()
        later(f"chip_send{n}", part_chip.at[n], chip_send.at[n])
        later(f"part{n}", part_chip.at[n], chip_recv.at[n])
    later("core_send", part_core, core_send)
    later("part", part_core, core_recv)

    finish("p_slots")
    p_to_pair = remote(p_own, p_pair, p_pair_send, p_pair_recv, pair)
    p_to_pair.start()
    later("p_pair_send", p_pair, p_pair_send)
    later("p_pair", p_pair, p_pair_recv)
    select = jnp.where(lane < 3 * experts, copies, 0.0)
    p_slot = dot(select.astype(BF16), p_own[...], NT)
    mine_row = iota((experts, cap), 0) == e
    p_mine = jnp.sum(jnp.where(mine_row, p_slot, 0.0), axis=0, keepdims=True)
    slope = p_mine * (jnp.where(mine_row, 1.0, 0.0) - p_slot)
    slope_row = dot(jnp.concatenate(thirds(slope), axis=0).astype(BF16), hot_own[...], NT)
    slope_row = slope_row[:experts] + slope_row[experts : 2 * experts] + slope_row[2 * experts :]
    finish("act_slots")
    act_row = dot(hot_own[...], act_own[...]).astype(BF16)

    wait_bytes(gate_two.at[pl.ds(0, SIDE - 1)], two_recv)
    total = jnp.sum(gate_two[...], axis=0)
    total_row = jnp.concatenate([total[k : k + 1, :] for k in range(2 * pieces)], axis=1)

    w_row = total_row * slope_row
    r_three = dot(jnp.concatenate(thirds(w_row), axis=0).astype(BF16), act_row)
    r_part = r_three[:experts] + r_three[experts : 2 * experts] + r_three[2 * experts :]
    r_out[...] = r_part.astype(BF16)
    for n, k in enumerate((middle, 2, -2, 1, -1)):
        remote(r_out, r_in.at[n], r_send, r_recv.at[min(n, 1)], at_z(k) * 2 + h).start()
    later("r_send", r_in.at[pl.ds(0, 5)], r_send)
    rows3 = jnp.concatenate([total_row, jnp.zeros((7, cap), F32)], axis=0)
    s_three = dot(jnp.concatenate(thirds(rows3), axis=0).astype(BF16), hot_own[...])
    s_slot = s_three[0:1] + s_three[8:9] + s_three[16:17]
    slot_at = iota((experts, cap), 1)
    of_owner = (jnp.right_shift(slot_at, slot_shift + 1) == iota((experts, cap), 0)) & (
        (jnp.right_shift(slot_at, slot_shift) & 1) == h
    )
    fold = jnp.where((iota((cap, LANES), 0) & (SLOTS - 1)) == iota((cap, LANES), 1), 1.0, 0.0)
    s_spread = jnp.concatenate(thirds(jnp.where(of_owner, s_slot, 0.0)), axis=0).astype(BF16)
    s_three = dot(s_spread, fold.astype(BF16))
    s_rows = s_three[:experts] + s_three[experts : 2 * experts] + s_three[2 * experts :]
    for k in range(experts):
        s_out[k] = s_rows[k : k + 1, :]

    for k in [middle] + [j * sign for j in range(middle - 1, 0, -1) for sign in (1, -1)]:
        remote(s_out.at[at_z(k) // 2], s_in.at[e], s_send, s_recv, at_z(k) * 2 + h).start()
    later("s_send", s_in.at[pl.ds(0, experts - 1)], s_send)
    later("s", s_in.at[pl.ds(0, experts - 1)], s_recv)
    s_in[e] = s_out[e]
    wait_bytes(r_in.at[pl.ds(1, 4)], r_recv.at[1])
    f_out[...] = r_part + sum(r_in[n].astype(F32) for n in range(1, 5))
    r_mid[...] = f_out[...].astype(BF16)
    for n, k in enumerate((5, -5)):
        remote(r_mid, r_in.at[5 + n], r_mid_send, r_recv.at[2], at_z(k) * 2 + h).start()
    later("r_mid_send", r_in.at[pl.ds(5, 2)], r_mid_send)

    finish("p_pair")
    gates = dot(hot_own[...], p_own[...]) + dot(hot_pair[...], p_pair[...])
    gate_col = jnp.sum(jnp.where(iota((cap, LANES), 1) == e, gates, 0.0), axis=1, keepdims=True)
    finish("part")
    finish("part0")
    finish("part1")
    pre = acc[0] + part_core[...] + (part_chip[0].astype(F32) + part_chip[1].astype(F32))
    hid_ref[...] = (gate_col * pre).astype(BF16)

    wait_bytes(r_in.at[0], r_recv.at[0])
    wait_bytes(r_in.at[pl.ds(5, 2)], r_recv.at[2])
    f_out[...] += r_in[0].astype(F32) + (r_in[5].astype(F32) + r_in[6].astype(F32))
    f_in[quarter] = f_out[...]
    for q in quarters:
        remote(f_out, f_in.at[quarter], f_send, f_recv, q).start()
    later("f_send", f_in.at[pl.ds(0, len(quarters))], f_send)

    finish("rw")
    finish("s")
    s_all = jnp.concatenate([s_in[k] for k in range(experts)], axis=0)
    unfold = jnp.where((iota((LANES, wide), 1) & (SLOTS - 1)) == iota((LANES, wide), 0), 1.0, 0.0)
    s_three = dot(jnp.concatenate(thirds(s_all), axis=0).astype(BF16), unfold.astype(BF16))
    s_sum = s_three[:experts] + s_three[experts : 2 * experts] + s_three[2 * experts :]
    own_lane = ((jnp.right_shift(iota((experts, wide), 1), slot_shift) + e) & (experts - 1)) == iota((experts, wide), 0)
    score3 = dot(jnp.concatenate(thirds(jnp.where(own_lane, s_sum, 0.0)), axis=0).astype(BF16), pick_bf, NT)
    score = score3[:experts] + score3[experts : 2 * experts] + score3[2 * experts :]
    inner = jnp.sum(probs * score, axis=0, keepdims=True)
    logit_grad = (probs * (score - inner)).astype(BF16)
    tok_ref[...] = dot(logit_grad, rw_ref[...], TN).astype(BF16)

    wait_bytes(f_in.at[pl.ds(0, len(quarters))], f_recv)
    rg_ref[:, :LANES] = f_in[0] + f_in[2]
    rg_ref[:, LANES:] = f_in[1] + f_in[3]

    for name in list(waits):
        finish(name)


def write(hid_ref, tok_ref, rg_ref, hid_out, tok_out, rg_out, sem):
    copies = [
        pltpu.make_async_copy(src, dst, sem.at[n])
        for n, (src, dst) in enumerate(((hid_ref, hid_out), (tok_ref, tok_out), (rg_ref, rg_out)))
    ]
    for copy in copies:
        copy.start()
    for copy in copies:
        copy.wait()


def on_device(
    cotangent, activations, router_logits, saved_hidden, down_weight, router_weight, choices
):
    experts, cap = choices.shape
    own_tokens, feats = cotangent.shape
    hidden = down_weight.shape[0]
    wide = experts * SLOTS
    blocks = SIDE * SIDE
    vmem = pl.BlockSpec(memory_space=pltpu.VMEM)
    hbm = pl.BlockSpec(memory_space=pltpu.HBM)
    dma = pltpu.SemaphoreType.DMA
    shapes = (
        jax.ShapeDtypeStruct((cap, hidden), BF16),
        jax.ShapeDtypeStruct((own_tokens, feats), BF16),
        jax.ShapeDtypeStruct((experts, feats), F32),
    )
    grads = pl.pallas_call(
        kernel,
        out_shape=shapes,
        in_specs=[hbm] * 7,
        out_specs=(vmem, vmem, vmem),
        scratch_shapes=[
            pltpu.VMEM((own_tokens, feats), BF16),
            pltpu.VMEM((own_tokens, feats), BF16),
            pltpu.VMEM((experts, own_tokens), F32),
            pltpu.VMEM((4, cap, hidden), BF16),
            pltpu.VMEM((experts, feats), BF16),
            pltpu.VMEM((experts, cap), I32),
            pltpu.VMEM((2, experts, SLOTS, LANES), BF16),
            pltpu.VMEM((2, experts, SLOTS, LANES), BF16),
            pltpu.VMEM((experts, SLOTS, LANES), BF16),
            pltpu.VMEM((4, 2 * SLOTS, LANES), BF16),
            pltpu.VMEM((4, 2 * SLOTS, LANES), BF16),
            pltpu.VMEM((cap, LANES), BF16),
            pltpu.VMEM((cap, LANES), BF16),
            pltpu.VMEM((cap, LANES), BF16),
            pltpu.VMEM((cap, LANES), BF16),
            pltpu.VMEM((cap, LANES), BF16),
            pltpu.VMEM((cap, cap), BF16),
            pltpu.VMEM((cap, cap), BF16),
            pltpu.VMEM((2 * SIDE, cap, LANES), BF16),
            pltpu.VMEM((4, 2 * SIDE, hidden, LANES), BF16),
            pltpu.VMEM((4, cap, hidden), F32),
            pltpu.VMEM((2, cap, hidden), BF16),
            pltpu.VMEM((cap, hidden), F32),
            pltpu.VMEM((2, cap, hidden), BF16),
            pltpu.VMEM((4 * SIDE, cap // LANES, LANES), F32),
            pltpu.VMEM((SIDE, cap // LANES, LANES), F32),
            pltpu.VMEM((experts, 1, LANES), F32),
            pltpu.VMEM((experts, 1, LANES), F32),
            pltpu.VMEM((experts, LANES), BF16),
            pltpu.VMEM((experts, LANES), BF16),
            pltpu.VMEM((7, experts, LANES), BF16),
            pltpu.VMEM((experts, LANES), F32),
            pltpu.VMEM((4, experts, LANES), F32),
            dma((6,)), dma(()), dma(()), dma((3,)), dma(()), dma((3,)),
            dma(()), dma((2, 4)), dma(()), dma(()), dma((experts,)), dma(()), dma(()),
            dma(()), dma(()), dma(()), dma(()), dma(()), dma(()), dma(()), dma(()),
            dma(()), dma((2, SIDE)), dma((2, 2, SIDE)), dma(()), dma(()), dma((2,)), dma((2,)),
            dma(()), dma(()), dma(()), dma(()),
            dma(()), dma(()), dma(()), dma(()), dma((3,)), dma(()), dma(()),
        ],
        compiler_params=pltpu.CompilerParams(
            collective_id=0, has_side_effects=True, vmem_limit_bytes=48 * 2**20
        ),
        cost_estimate=pl.CostEstimate(
            flops=2 * cap * hidden * feats * blocks, bytes_accessed=4 * 2**20, transcendentals=0
        ),
        name="gated_moe_backward",
    )(
        *(
            pltpu.with_memory_space_constraint(v, pltpu.HBM)
            for v in (
                cotangent, activations, router_logits.T, saved_hidden, down_weight, router_weight.T, choices
            )
        )
    )
    hidden_grad, token_grad, router_grad = pl.pallas_call(
        write,
        out_shape=shapes,
        in_specs=[vmem] * 3,
        out_specs=(hbm, hbm, hbm),
        scratch_shapes=[dma((3,))],
        compiler_params=pltpu.CompilerParams(vmem_limit_bytes=2 * 2**20),
        name="write_gradients",
    )(*grads)
    return hidden_grad, token_grad, router_grad.T


def solution(mesh):
    placed = (
        P("expert", "tensor"),
        P("expert", "tensor"),
        P("expert", None),
        P(None, ("expert", "tensor")),
        P(("expert", "tensor"), None),
        P("tensor", None),
        P(),
    )
    return jax.shard_map(
        on_device,
        mesh=mesh,
        in_specs=placed,
        out_specs=(P(None, ("expert", "tensor")), P("expert", "tensor"), P("tensor", None)),
        check_vma=False,
    )
```

```python
import functools

import jax
import jax.numpy as jnp
from jax import lax
from jax.experimental import pallas as pl
from jax.experimental.pallas import tpu as pltpu
from jax.sharding import PartitionSpec as P

MESH = pl.DeviceIdType.MESH
F32 = jnp.float32
BF16 = jnp.bfloat16
I32 = jnp.int32
SLOTS = 16
SIDE = 4
LANES = 128
NT = (((1,), (1,)), ((), ()))
TN = (((0,), (0,)), ((), ()))
NN = (((1,), (0,)), ((), ()))


def iota(shape, axis):
    return lax.broadcasted_iota(I32, shape, axis)


def dot(a, b, dims=NN, precision=None):
    return lax.dot_general(a, b, dims, precision=precision, preferred_element_type=F32)


def exact(a, b, dims=NN):
    return dot(a, b, dims, lax.Precision.HIGHEST)


def thirds(v):
    a = v.astype(BF16).astype(F32)
    b = (v - a).astype(BF16).astype(F32)
    return a, b, v - a - b


def shift_of(n):
    return n.bit_length() - 1


def kernel(
    cot_hbm, act_hbm, logit_hbm, saved_hbm, w_hbm, rw_hbm, choice_hbm,
    hid_ref, tok_ref, rg_ref,
    cot_ref, act_ref, logit_ref, saved, rw_ref, choice_ref,
    cot_out, act_out, p_out, up, down, cot_own, cot_pair, act_own, p_own, p_pair,
    hot_own, hot_pair, xbuf, weights, acc, acc_out, part_core, part_chip,
    gate_one, gate_two, s_out, s_in, r_out, r_mid, r_in, f_out, f_in,
    in_sem, w_sem, w_send, w_recv, saved_send, saved_recv,
    up_send, up_recv, near_send, hop_send, cot_recv, pair_send, pair_recv,
    act_send, act_recv, p_send, p_recv, p_two_send, p_two_recv, p_pair_send, p_pair_recv,
    x_send, x_one, x_two, core_send, core_recv, chip_send, chip_recv, one_send, one_recv, two_send, two_recv,
    s_send, s_recv, r_send, r_mid_send, r_recv, f_send, f_recv,
):
    me, xy = lax.axis_index("expert"), lax.axis_index("tensor")
    groups = lax.axis_size("expert")
    chips = groups // 2
    experts, cap = choice_ref.shape
    own_tokens, feats = cot_ref.shape
    z, h = me // 2, me % 2
    e = z // 2
    x, y = xy // SIDE, xy % SIDE
    other_core = z * 2 + (1 - h)
    beside = x + 1 - 2 * (x % 2)
    beside_xy = beside * SIDE + y
    mirror_xy = (SIDE - 1 - x) * SIDE + y
    pair_z = z + 1 - 2 * (z % 2)
    pair = pair_z * 2 + h
    quarter = (z % 2) * 2 + h
    quarters = (other_core, pair, pair_z * 2 + (1 - h))
    far = 4
    token_shift, slot_shift = shift_of(own_tokens), shift_of(SLOTS)

    def remote(src, dst, send, recv, expert_at, tensor_at=xy):
        return pltpu.make_async_remote_copy(
            src_ref=src, dst_ref=dst, send_sem=send, recv_sem=recv,
            device_id=(expert_at, tensor_at), device_id_type=MESH,
        )

    def wait_bytes(ref, sem):
        pltpu.make_async_copy(ref, ref, sem).wait()

    waits = {}

    def later(name, ref, sem):
        waits[name] = lambda: wait_bytes(ref, sem)

    def finish(name):
        waits.pop(name)()

    def at_xy(i, j):
        return ((x + i) % SIDE) * SIDE + (y + j) % SIDE

    def at_z(k):
        return (z + 2 * k + 2 * chips) % chips

    arrays = {
        "choice": (choice_hbm, choice_ref), "cot": (cot_hbm, cot_ref), "act": (act_hbm, act_ref),
        "logit": (logit_hbm, logit_ref), "saved": (saved_hbm, saved.at[0]), "rw": (rw_hbm, rw_ref),
    }

    def load(*names):
        for name in names:
            src, dst = arrays[name]
            sem = in_sem.at[list(arrays).index(name)]
            pltpu.make_async_copy(src, dst, sem).start()
            later(name, dst, sem)

    load("choice", "cot")

    barrier = pltpu.get_barrier_semaphore()

    def greet(expert_at, tensor_at):
        pl.semaphore_signal(barrier, inc=1, device_id=(expert_at, tensor_at), device_id_type=MESH)

    near_steps = [k * sign for k in range(far, 0, -1) for sign in (1, -1)]
    for k in near_steps:
        for c in range(2):
            greet(at_z(k) * 2 + c, xy)
    for i in range(1, SIDE):
        greet(me, at_xy(0, i))
        greet(me, at_xy(i, 0))
        for q in quarters:
            greet(q, at_xy(i, 0))
    for q in quarters:
        greet(q, xy)
    greeted = 2 * len(near_steps) + 5 * (SIDE - 1) + len(quarters)

    finish("choice")
    tokens_at = iota((own_tokens, cap), 0) + me * own_tokens
    lane_expert = iota((own_tokens, LANES), 1)
    chosen = jnp.zeros((own_tokens, LANES), F32)
    for n in range(experts):
        hit = jnp.where(choice_ref[n : n + 1, :] == tokens_at, 1.0, 0.0)
        chosen = jnp.where(lane_expert == n, jnp.sum(hit, axis=1, keepdims=True), chosen)
    before = (iota((own_tokens, own_tokens), 1) < iota((own_tokens, own_tokens), 0)).astype(F32).astype(BF16)
    place = dot(before, chosen.astype(BF16))
    wide = experts * SLOTS
    group_of = (jnp.right_shift(iota((LANES, wide), 1), slot_shift) + e) & (experts - 1)
    spread = (group_of == iota((LANES, wide), 0)).astype(F32).astype(BF16)
    chosen_wide = dot(chosen.astype(BF16), spread)
    place_wide = dot(place.astype(BF16), spread)
    slot_lane = (iota((own_tokens, wide), 1) & (SLOTS - 1)).astype(F32)
    pick = jnp.where((chosen_wide > 0.5) & (place_wide == slot_lane), 1.0, 0.0)
    pick_bf = pick.astype(BF16)
    finish("cot")
    cot_slots = dot(pick_bf, cot_ref[...], TN).astype(BF16)
    cot_out[0] = cot_slots[:, :LANES].reshape(experts, SLOTS, LANES)
    cot_out[1] = cot_slots[:, LANES:].reshape(experts, SLOTS, LANES)

    pl.semaphore_wait(barrier, greeted)

    slots_of_core = pl.ds(pl.multiple_of(h * SLOTS, SLOTS), SLOTS)

    def relay_up(c, j):
        remote(
            cot_out.at[c, far + 1 + j], up.at[j, slots_of_core], up_send, up_recv.at[0, j], at_z(far) * 2 + c
        ).start()

    def relay_down(c, j):
        remote(
            cot_out.at[c, 2 * far + j], down.at[j, slots_of_core], up_send, up_recv.at[1, j], at_z(-far) * 2 + c
        ).start()

    pair_rows = 2 * SLOTS

    def rows_from(k):
        return pl.ds(pl.multiple_of(((e - k + experts) % experts) * pair_rows, pair_rows), pair_rows)

    mine = pl.ds(pl.multiple_of(e * pair_rows + h * SLOTS, SLOTS), SLOTS)
    for k in near_steps:
        for c in range(2):
            remote(
                cot_out.at[c, k % experts], cot_own.at[mine], near_send, cot_recv.at[k % experts], at_z(k) * 2 + c
            ).start()
    relay_up(0, far - 1)
    relay_down(1, 0)
    for j in range(1, far):
        for c in range(2):
            relay_up(c, far - 1 - j)
            relay_down(c, j)
    remote(cot_out.at[1 - h, 0], cot_own.at[mine], near_send, cot_recv.at[0], other_core).start()
    pltpu.make_async_copy(cot_out.at[h, 0], cot_own.at[mine], cot_recv.at[0]).start()
    later("near", cot_own.at[pl.ds(0, (2 * len(near_steps) + 1) * SLOTS)], near_send)

    def half_of(px, c, j):
        return w_hbm.at[:, pl.ds(pl.multiple_of((px * SIDE + j) * 2 * LANES + c * LANES, LANES), LANES)]

    load("act", "logit", "saved", "rw")
    for p, px in enumerate((x, SIDE - 1 - x)):
        for j in range(SIDE):
            pltpu.make_async_copy(half_of(px, h, j), weights.at[0, p * SIDE + j], w_sem).start()
    for p, px in enumerate((beside, SIDE - 1 - beside)):
        for j in range(SIDE):
            at = p * SIDE + j
            remote(half_of(px, h, j), weights.at[2, at], w_send, w_recv.at[1], me, beside_xy).start()
            remote(half_of(px, 1 - h, j), weights.at[3, at], w_send, w_recv.at[2], other_core, beside_xy).start()
    for p, px in enumerate((x, SIDE - 1 - x)):
        for j in range(SIDE):
            remote(half_of(px, 1 - h, j), weights.at[1, p * SIDE + j], w_send, w_recv.at[0], other_core).start()
    remote(saved_hbm, saved.at[2], saved_send, saved_recv.at[1], me, beside_xy).start()
    remote(saved_hbm, saved.at[1], saved_send, saved_recv.at[0], other_core).start()
    later("w0", weights.at[0], w_sem)
    later("w_send", weights.at[pl.ds(0, 3)], w_send)
    later("saved_send", saved.at[pl.ds(0, 3)], saved_send)
    for n in range(3):
        later(f"w{n + 1}", weights.at[n + 1], w_recv.at[n])
        later(f"saved{n + 1}", saved.at[n + 1], saved_recv.at[n])

    finish("act")
    act_slots = dot(pick_bf, act_ref[...], TN).astype(BF16)
    act_out[0] = act_slots[:, :LANES].reshape(experts, SLOTS, LANES)
    act_out[1] = act_slots[:, LANES:].reshape(experts, SLOTS, LANES)
    finish("logit")
    logits = logit_ref[...]
    grown = jnp.exp(logits - jnp.max(logits, axis=0, keepdims=True))
    probs = grown / jnp.sum(grown, axis=0, keepdims=True)
    lane = iota((experts, LANES), 1)
    copies = jnp.where((lane & (experts - 1)) == iota((experts, LANES), 0), 1.0, 0.0)
    p_terms = thirds(exact(probs, copies, TN))
    term = jnp.right_shift(iota((own_tokens, LANES), 1), shift_of(experts))
    p_wide = jnp.where(
        term == 0, p_terms[0], jnp.where(term == 1, p_terms[1], jnp.where(term == 2, p_terms[2], 0.0))
    )
    p_out[...] = dot(pick_bf, p_wide.astype(BF16), TN).astype(BF16).reshape(experts, SLOTS, LANES)

    middle = experts // 2

    def act_to(k):
        for c in range(2):
            remote(act_out.at[c, k], act_own.at[mine], act_send, act_recv, at_z(k) * 2 + c).start()

    def act_each(j, carry):
        act_to(middle - j)
        act_to(middle + j)
        return carry

    def p_to(k):
        for c in range(2):
            remote(p_out.at[k], p_own.at[mine], p_send, p_recv, at_z(k) * 2 + c).start()

    def send_rest():
        act_to(middle)
        lax.fori_loop(1, middle, act_each, 0)
        remote(act_out.at[1 - h, 0], act_own.at[mine], act_send, act_recv, other_core).start()
        pltpu.make_async_copy(act_out.at[h, 0], act_own.at[mine], act_recv).start()
        later("act_send", act_own.at[pl.ds(0, cap - SLOTS)], act_send)
        later("act_slots", act_own, act_recv)
        waits["p_send"] = p_sent

    def send_p():
        for m in range(SIDE - 1, 0, -1):
            p_to(m * SIDE + y)

        @pl.when(y != 0)
        def _():
            p_to(y)

        @pl.when(y == 0)
        def _():
            remote(p_out.at[0], p_own.at[mine], p_send, p_recv, other_core).start()
            pltpu.make_async_copy(p_out.at[0], p_own.at[mine], p_recv).start()

    def p_sent():
        sends = 2 * experts // SIDE

        @pl.when(y == 0)
        def _():
            wait_bytes(p_own.at[pl.ds(0, (sends - 1) * SLOTS)], p_send)

        @pl.when(y != 0)
        def _():
            wait_bytes(p_own.at[pl.ds(0, sends * SLOTS)], p_send)

    def share_p():
        wait_bytes(p_own.at[pl.ds(0, cap // SIDE)], p_recv)
        for m in range(SIDE):
            rows = rows_from(m * SIDE + y)
            for j in (2, 1, 3):
                remote(p_own.at[rows], p_own.at[rows], p_two_send, p_two_recv, me, at_xy(0, j)).start()
        rest = p_own.at[pl.ds(0, cap - cap // SIDE)]
        later("p_two_send", rest, p_two_send)
        later("p_slots", rest, p_two_recv)

    def share(k):
        rows = rows_from(k)
        wait_bytes(cot_own.at[rows], cot_recv.at[k % experts])
        remote(cot_own.at[rows], cot_pair.at[rows], pair_send, pair_recv, pair).start()

    later("pair_send", cot_pair, pair_send)
    later("pair", cot_pair, pair_recv)

    def hop_up(j):
        wait_bytes(up.at[j], up_recv.at[0, j])
        remote(
            up.at[j], cot_own.at[rows_from(far)], hop_send, cot_recv.at[far + 1 + j], at_z(1 + j) * 2 + h
        ).start()

    def hop_down(j):
        wait_bytes(down.at[j], up_recv.at[1, j])
        remote(
            down.at[j], cot_own.at[rows_from(-far)], hop_send, cot_recv.at[2 * far + j], at_z(j - far) * 2 + h
        ).start()

    for k in (0, 1, -1, 2, -2):
        share(k)
    @pl.when(h == 0)
    def _():
        hop_up(far - 1)

    @pl.when(h == 1)
    def _():
        hop_down(0)

    for j in range(1, far):
        hop_up(far - 1 - j)
        hop_down(j)
    relayed = cot_own.at[pl.ds(0, 2 * (2 * far - 1) * SLOTS)]
    send_p()
    later("up_send", relayed, up_send)
    later("hop_send", relayed, hop_send)

    wanted = choice_ref[pl.ds(e, 1), :].astype(F32)
    wanted_col = jnp.transpose(jnp.broadcast_to(wanted, (LANES, cap)))[:, :1].astype(I32)
    wanted_row = wanted.astype(I32)
    owner_col = jnp.right_shift(wanted_col, token_shift)
    owner_row = jnp.right_shift(wanted_row, token_shift)
    earlier = (owner_row == owner_col) & (wanted_row < wanted_col)
    rank = jnp.sum(jnp.where(earlier, 1.0, 0.0), axis=1, keepdims=True).astype(I32)
    slot = jnp.right_shift(owner_col, 2) * pair_rows + (owner_col & 1) * SLOTS + rank
    ours = (jnp.right_shift(owner_col, 1) & 1) == z % 2
    slot_lanes = iota((cap, cap), 1)
    hot_own[...] = jnp.where(jnp.where(ours, slot, -1) == slot_lanes, 1.0, 0.0).astype(BF16)
    hot_pair[...] = jnp.where(jnp.where(ours, -1, slot) == slot_lanes, 1.0, 0.0).astype(BF16)

    for k in (3, -3, 4, -4, 5, -5, 6, -6, 7, -7, 8):
        share(k)
    half = cap // 2
    picked = dot(hot_own[...], cot_own[...])
    finish("pair")

    order = (1, 3, 2)

    def rows_of(first):
        return pl.ds(first * half, half)

    def send_block(first, src, dst, recv, to):
        remote(xbuf.at[src, rows_of(first)], xbuf.at[dst, rows_of(first)], x_send, recv, me, to).start()

    def from_y(j):
        return (y - j + SIDE) % SIDE

    for first in range(2):
        rows = slice(first * half, (first + 1) * half)
        xbuf[y, rows_of(first), :] = (picked[rows] + dot(hot_pair[rows, :], cot_pair[...])).astype(BF16)
        if first == 0:
            send_block(0, y, SIDE + y, x_one.at[0, 0], mirror_xy)
        else:
            for j in order:
                send_block(1, y, y, x_one.at[1, j], at_xy(0, j))
    for j in order:
        send_block(0, y, y, x_two.at[0, 0, j], at_xy(0, j))
    send_block(1, y, SIDE + y, x_two.at[1, 0, 0], mirror_xy)
    later("x_send", xbuf.at[pl.ds(0, 2 * SIDE - 1)], x_send)
    send_rest()
    wait_bytes(xbuf.at[SIDE + y, rows_of(0)], x_one.at[0, 0])
    for j in order:
        send_block(0, SIDE + y, SIDE + y, x_two.at[0, 1, j], at_xy(0, j))
    for j in order:
        wait_bytes(xbuf.at[from_y(j), rows_of(1)], x_one.at[1, j])
        send_block(1, from_y(j), SIDE + from_y(j), x_two.at[1, 0, j], mirror_xy)
    share_p()
    finish("saved2")
    remote(saved.at[2], saved.at[3], saved_send, saved_recv.at[2], other_core).start()
    for n in range(4):
        finish(f"w{n}")

    def product(p, first, n):
        blocks_at = range(p * SIDE, (p + 1) * SIDE)
        lhs = jnp.concatenate([xbuf[b, first * half : (first + 1) * half, :] for b in blocks_at], axis=1)
        rhs = jnp.concatenate([weights[n, b] for b in blocks_at], axis=1)
        return dot(lhs, rhs, NT)

    def span(first):
        return slice(first * half, (first + 1) * half)

    for j in order:
        wait_bytes(xbuf.at[from_y(j), rows_of(0)], x_two.at[0, 0, j])
    for first in range(2):
        for n in range(4):
            acc[n, span(first), :] = product(0, first, n)
    finish("saved")
    finish("saved1")
    finish("saved3")
    slot_one = x * 4 + quarter
    pieces = half // LANES
    for first in range(2):
        for j in order if first == 0 else (0, *order):
            sem = x_two.at[0, 1, j] if first == 0 else x_two.at[1, 0, j]
            wait_bytes(xbuf.at[SIDE + from_y(j), rows_of(first)], sem)
        prod = 0.0
        for n in range(4):
            pre = acc[n, span(first), :] + product(1, first, n)
            acc[n, span(first), :] = pre
            prod += saved[n, span(first), :].astype(F32) * pre
        gate = jnp.sum(jnp.transpose(prod[:, :LANES] + prod[:, LANES:]), axis=0, keepdims=True)
        for k in range(pieces):
            gate_one[slot_one, first * pieces + k : first * pieces + k + 1, :] = gate[:, k * LANES : (k + 1) * LANES]

    for i in (2, 1, 3, 0):
        for q in quarters + (() if i == 0 else (me,)):
            remote(gate_one.at[slot_one], gate_one.at[slot_one], one_send, one_recv, q, at_xy(i, 0)).start()
    later("one_send", gate_one.at[pl.ds(0, 4 * SIDE - 1)], one_send)
    wait_bytes(gate_one.at[pl.ds(0, 4 * SIDE - 1)], one_recv)
    gate_two[y] = jnp.sum(gate_one[...], axis=0)
    for j in (2, 1, 3):
        remote(gate_two.at[y], gate_two.at[y], two_send, two_recv, me, at_xy(0, j)).start()
    later("two_send", gate_two.at[pl.ds(0, SIDE - 1)], two_send)

    remote(acc.at[1], part_core, core_send, core_recv, other_core).start()
    for n, to in enumerate((me, other_core)):
        acc_out[n] = acc[2 + n].astype(BF16)
        remote(acc_out.at[n], part_chip.at[n], chip_send.at[n], chip_recv.at[n], to, beside_xy).start()
        later(f"chip_send{n}", part_chip.at[n], chip_send.at[n])
        later(f"part{n}", part_chip.at[n], chip_recv.at[n])
    later("core_send", part_core, core_send)
    later("part", part_core, core_recv)

    finish("p_slots")
    p_to_pair = remote(p_own, p_pair, p_pair_send, p_pair_recv, pair)
    p_to_pair.start()
    later("p_pair_send", p_pair, p_pair_send)
    later("p_pair", p_pair, p_pair_recv)
    select = jnp.where(lane < 3 * experts, copies, 0.0)
    p_slot = dot(select.astype(BF16), p_own[...], NT)
    mine_row = iota((experts, cap), 0) == e
    p_mine = jnp.sum(jnp.where(mine_row, p_slot, 0.0), axis=0, keepdims=True)
    slope = p_mine * (jnp.where(mine_row, 1.0, 0.0) - p_slot)
    slope_row = dot(jnp.concatenate(thirds(slope), axis=0).astype(BF16), hot_own[...], NT)
    slope_row = slope_row[:experts] + slope_row[experts : 2 * experts] + slope_row[2 * experts :]
    finish("act_slots")
    act_row = dot(hot_own[...], act_own[...]).astype(BF16)

    wait_bytes(gate_two.at[pl.ds(0, SIDE - 1)], two_recv)
    total = jnp.sum(gate_two[...], axis=0)
    total_row = jnp.concatenate([total[k : k + 1, :] for k in range(2 * pieces)], axis=1)

    w_row = total_row * slope_row
    r_three = dot(jnp.concatenate(thirds(w_row), axis=0).astype(BF16), act_row)
    r_part = r_three[:experts] + r_three[experts : 2 * experts] + r_three[2 * experts :]
    r_out[...] = r_part.astype(BF16)
    for n, k in enumerate((middle, 2, -2, 1, -1)):
        remote(r_out, r_in.at[n], r_send, r_recv.at[min(n, 1)], at_z(k) * 2 + h).start()
    later("r_send", r_in.at[pl.ds(0, 5)], r_send)
    rows3 = jnp.concatenate([total_row, jnp.zeros((7, cap), F32)], axis=0)
    s_three = dot(jnp.concatenate(thirds(rows3), axis=0).astype(BF16), hot_own[...])
    s_slot = s_three[0:1] + s_three[8:9] + s_three[16:17]
    slot_at = iota((experts, cap), 1)
    of_owner = (jnp.right_shift(slot_at, slot_shift + 1) == iota((experts, cap), 0)) & (
        (jnp.right_shift(slot_at, slot_shift) & 1) == h
    )
    fold = jnp.where((iota((cap, LANES), 0) & (SLOTS - 1)) == iota((cap, LANES), 1), 1.0, 0.0)
    s_spread = jnp.concatenate(thirds(jnp.where(of_owner, s_slot, 0.0)), axis=0).astype(BF16)
    s_three = dot(s_spread, fold.astype(BF16))
    s_rows = s_three[:experts] + s_three[experts : 2 * experts] + s_three[2 * experts :]
    for k in range(experts):
        s_out[k] = s_rows[k : k + 1, :]

    for k in [middle] + [j * sign for j in range(middle - 1, 0, -1) for sign in (1, -1)]:
        remote(s_out.at[at_z(k) // 2], s_in.at[e], s_send, s_recv, at_z(k) * 2 + h).start()
    later("s_send", s_in.at[pl.ds(0, experts - 1)], s_send)
    later("s", s_in.at[pl.ds(0, experts - 1)], s_recv)
    s_in[e] = s_out[e]
    wait_bytes(r_in.at[pl.ds(1, 4)], r_recv.at[1])
    f_out[...] = r_part + sum(r_in[n].astype(F32) for n in range(1, 5))
    r_mid[...] = f_out[...].astype(BF16)
    for n, k in enumerate((5, -5)):
        remote(r_mid, r_in.at[5 + n], r_mid_send, r_recv.at[2], at_z(k) * 2 + h).start()
    later("r_mid_send", r_in.at[pl.ds(5, 2)], r_mid_send)

    finish("p_pair")
    gates = dot(hot_own[...], p_own[...]) + dot(hot_pair[...], p_pair[...])
    gate_col = jnp.sum(jnp.where(iota((cap, LANES), 1) == e, gates, 0.0), axis=1, keepdims=True)
    finish("part")
    finish("part0")
    finish("part1")
    pre = acc[0] + part_core[...] + (part_chip[0].astype(F32) + part_chip[1].astype(F32))
    hid_ref[...] = (gate_col * pre).astype(BF16)

    wait_bytes(r_in.at[0], r_recv.at[0])
    wait_bytes(r_in.at[pl.ds(5, 2)], r_recv.at[2])
    f_out[...] += r_in[0].astype(F32) + (r_in[5].astype(F32) + r_in[6].astype(F32))
    f_in[quarter] = f_out[...]
    for q in quarters:
        remote(f_out, f_in.at[quarter], f_send, f_recv, q).start()
    later("f_send", f_in.at[pl.ds(0, len(quarters))], f_send)

    finish("rw")
    finish("s")
    s_all = jnp.concatenate([s_in[k] for k in range(experts)], axis=0)
    unfold = jnp.where((iota((LANES, wide), 1) & (SLOTS - 1)) == iota((LANES, wide), 0), 1.0, 0.0)
    s_three = dot(jnp.concatenate(thirds(s_all), axis=0).astype(BF16), unfold.astype(BF16))
    s_sum = s_three[:experts] + s_three[experts : 2 * experts] + s_three[2 * experts :]
    own_lane = ((jnp.right_shift(iota((experts, wide), 1), slot_shift) + e) & (experts - 1)) == iota((experts, wide), 0)
    score3 = dot(jnp.concatenate(thirds(jnp.where(own_lane, s_sum, 0.0)), axis=0).astype(BF16), pick_bf, NT)
    score = score3[:experts] + score3[experts : 2 * experts] + score3[2 * experts :]
    inner = jnp.sum(probs * score, axis=0, keepdims=True)
    logit_grad = (probs * (score - inner)).astype(BF16)
    tok_ref[...] = dot(logit_grad, rw_ref[...], TN).astype(BF16)

    wait_bytes(f_in.at[pl.ds(0, len(quarters))], f_recv)
    rg_ref[:, :LANES] = f_in[0] + f_in[2]
    rg_ref[:, LANES:] = f_in[1] + f_in[3]

    for name in list(waits):
        finish(name)


def write(hid_ref, tok_ref, rg_ref, hid_out, tok_out, rg_out, sem):
    copies = [
        pltpu.make_async_copy(src, dst, sem.at[n])
        for n, (src, dst) in enumerate(((hid_ref, hid_out), (tok_ref, tok_out), (rg_ref, rg_out)))
    ]
    for copy in copies:
        copy.start()
    for copy in copies:
        copy.wait()


def on_device(
    cotangent, activations, router_logits, saved_hidden, down_weight, router_weight, choices
):
    experts, cap = choices.shape
    own_tokens, feats = cotangent.shape
    hidden = down_weight.shape[0]
    wide = experts * SLOTS
    blocks = SIDE * SIDE
    vmem = pl.BlockSpec(memory_space=pltpu.VMEM)
    hbm = pl.BlockSpec(memory_space=pltpu.HBM)
    dma = pltpu.SemaphoreType.DMA
    shapes = (
        jax.ShapeDtypeStruct((cap, hidden), BF16),
        jax.ShapeDtypeStruct((own_tokens, feats), BF16),
        jax.ShapeDtypeStruct((experts, feats), F32),
    )
    grads = pl.pallas_call(
        kernel,
        out_shape=shapes,
        in_specs=[hbm] * 7,
        out_specs=(vmem, vmem, vmem),
        scratch_shapes=[
            pltpu.VMEM((own_tokens, feats), BF16),
            pltpu.VMEM((own_tokens, feats), BF16),
            pltpu.VMEM((experts, own_tokens), F32),
            pltpu.VMEM((4, cap, hidden), BF16),
            pltpu.VMEM((experts, feats), BF16),
            pltpu.VMEM((experts, cap), I32),
            pltpu.VMEM((2, experts, SLOTS, LANES), BF16),
            pltpu.VMEM((2, experts, SLOTS, LANES), BF16),
            pltpu.VMEM((experts, SLOTS, LANES), BF16),
            pltpu.VMEM((4, 2 * SLOTS, LANES), BF16),
            pltpu.VMEM((4, 2 * SLOTS, LANES), BF16),
            pltpu.VMEM((cap, LANES), BF16),
            pltpu.VMEM((cap, LANES), BF16),
            pltpu.VMEM((cap, LANES), BF16),
            pltpu.VMEM((cap, LANES), BF16),
            pltpu.VMEM((cap, LANES), BF16),
            pltpu.VMEM((cap, cap), BF16),
            pltpu.VMEM((cap, cap), BF16),
            pltpu.VMEM((2 * SIDE, cap, LANES), BF16),
            pltpu.VMEM((4, 2 * SIDE, hidden, LANES), BF16),
            pltpu.VMEM((4, cap, hidden), F32),
            pltpu.VMEM((2, cap, hidden), BF16),
            pltpu.VMEM((cap, hidden), F32),
            pltpu.VMEM((2, cap, hidden), BF16),
            pltpu.VMEM((4 * SIDE, cap // LANES, LANES), F32),
            pltpu.VMEM((SIDE, cap // LANES, LANES), F32),
            pltpu.VMEM((experts, 1, LANES), F32),
            pltpu.VMEM((experts, 1, LANES), F32),
            pltpu.VMEM((experts, LANES), BF16),
            pltpu.VMEM((experts, LANES), BF16),
            pltpu.VMEM((7, experts, LANES), BF16),
            pltpu.VMEM((experts, LANES), F32),
            pltpu.VMEM((4, experts, LANES), F32),
            dma((6,)), dma(()), dma(()), dma((3,)), dma(()), dma((3,)),
            dma(()), dma((2, 4)), dma(()), dma(()), dma((experts,)), dma(()), dma(()),
            dma(()), dma(()), dma(()), dma(()), dma(()), dma(()), dma(()), dma(()),
            dma(()), dma((2, SIDE)), dma((2, 2, SIDE)), dma(()), dma(()), dma((2,)), dma((2,)),
            dma(()), dma(()), dma(()), dma(()),
            dma(()), dma(()), dma(()), dma(()), dma((3,)), dma(()), dma(()),
        ],
        compiler_params=pltpu.CompilerParams(
            collective_id=0, has_side_effects=True, vmem_limit_bytes=48 * 2**20
        ),
        cost_estimate=pl.CostEstimate(
            flops=2 * cap * hidden * feats * blocks, bytes_accessed=4 * 2**20, transcendentals=0
        ),
        name="gated_moe_backward",
    )(
        *(
            pltpu.with_memory_space_constraint(v, pltpu.HBM)
            for v in (
                cotangent, activations, router_logits.T, saved_hidden, down_weight, router_weight.T, choices
            )
        )
    )
    hidden_grad, token_grad, router_grad = pl.pallas_call(
        write,
        out_shape=shapes,
        in_specs=[vmem] * 3,
        out_specs=(hbm, hbm, hbm),
        scratch_shapes=[dma((3,))],
        compiler_params=pltpu.CompilerParams(vmem_limit_bytes=2 * 2**20),
        name="write_gradients",
    )(*grads)
    return hidden_grad, token_grad, router_grad.T


def solution(mesh):
    placed = (
        P("expert", "tensor"),
        P("expert", "tensor"),
        P("expert", None),
        P(None, ("expert", "tensor")),
        P(("expert", "tensor"), None),
        P("tensor", None),
        P(),
    )
    return jax.shard_map(
        on_device,
        mesh=mesh,
        in_specs=placed,
        out_specs=(P(None, ("expert", "tensor")), P("expert", "tensor"), P("tensor", None)),
        check_vma=False,
    )
```
